32 devices in a mesh: dp: 8 (over z, core), expert: 4 (over y, x).
Axes of the slice: x: 2, y: 2, z: 4, core: 2. Of those that a mesh axis runs over, the one named last changes fastest.
Arguments:
- tokens: bfloat16 [16384, 512], P(('dp', 'expert')), may hold values from -6 to 6
- segments: int32 [16384], P(('dp', 'expert')), may hold values from -1 to 9, as said below
- experts: int32 [16384, 2], P(('dp', 'expert')), may hold values from 0 to 7, all different within a row; in each aligned block of 512 rows (0 to 511, 512 to 1023, ...) at most 192 rows name the same one
- priority: int32 [16384, 2], P(('dp', 'expert')), may hold values from 0 to 4095, as said below
- cotangent: bfloat16 [16384, 512], P(('dp', 'expert')), may hold values from -6 to 6
- ln1_gain: float32 [512], replicated, may hold values from 0.5 to 1.5
- ln1_bias: float32 [512], replicated, may hold values from -1 to 1
- w_qkv: bfloat16 [512, 1536], replicated, may hold values from -0.25 to 0.25
- w_attn_out: bfloat16 [512, 512], replicated, may hold values from -2 to 2
- ln2_gain: float32 [512], replicated, may hold values from 0.5 to 1.5
- ln2_bias: float32 [512], replicated, may hold values from -1 to 1
- w_up: bfloat16 [512, 2048], replicated, may hold values from -0.25 to 0.25
- w_down: bfloat16 [2048, 512], replicated, may hold values from -0.125 to 0.125
- ln3_gain: float32 [512], replicated, may hold values from 0.5 to 1.5
- ln3_bias: float32 [512], replicated, may hold values from -1 to 1
- w_router: bfloat16 [512, 8], replicated, may hold values from -0.1875 to 0.1875
- expert_up: bfloat16 [8, 512, 2048], P('expert'), may hold values from -0.25 to 0.25
- expert_down: bfloat16 [8, 2048, 512], P('expert'), may hold values from -1.5 to 1.5
Outputs:
- output: bfloat16 [16384, 512], P(('dp', 'expert'))
- grad_tokens: float32 [16384, 512], P(('dp', 'expert'))
- grad_ln1_gain: float32 [512], P('expert')
- grad_ln1_bias: float32 [512], P('expert')
- grad_qkv: float32 [512, 1536], P('expert')
- grad_attn_out: float32 [512, 512], P('expert')
- grad_ln2_gain: float32 [512], P('expert')
- grad_ln2_bias: float32 [512], P('expert')
- grad_up: float32 [512, 2048], P('expert')
- grad_down: float32 [2048, 512], P('expert')
- grad_ln3_gain: float32 [512], P('expert')
- grad_ln3_bias: float32 [512], P('expert')
- grad_router: float32 [512, 8], P('expert')
- grad_expert_up: float32 [8, 512, 2048], P('expert', 'dp')
- grad_expert_down: float32 [8, 2048, 512], P('expert', 'dp')
- expert_counts: float32 [8, 2], P('expert')
The draws below stay inside these ranges and needn't reach their ends.
Inputs may be any that keep to these rules, and one draw needn't show every extreme that they name: `segments`: each sequence of 512 slots holds whole images of 49 or 144 patches in order, numbered from 0 in the sequence; the slots after the last whole image are padding, numbered -1. Some sequence holds only images of 49 patches. A token names 2 different experts. Among the tokens of one device no expert is named more than 192 times, and on some device one expert exactly 192 times. `priority`: within a routing batch the 4096 ranks are distinct, and every first choice ranks above every second choice.
All inputs are finite; a program needn't handle non-finite values.
Results may differ from the reference program's by a relative error of at most 0.023.
Values may be sent and summed in bfloat16 or wider, within the bound.
A program may use at most 192 MiB of HBM per device.

```python
import math
import jax
import jax.numpy as jnp
import numpy as np
from jax import lax

D = 512
HEADS = 8
HD = 64
FF = 2048
TOP = 2
SEQ = 512
IMG_A = 49
IMG_B = 144
E = 8
TOK_DEV = 512
GROUP_TOK = 2048
GROUPS = 8
TOKENS = 16384
MOST = 192
CAP = 538


def draw_segments(key, part):
    key = jax.random.fold_in(key, 7)
    pick_key, row_key = jax.random.split(key)
    image_slots = SEQ // IMG_A + 1
    seq_total = TOKENS // SEQ
    picks = jax.random.randint(pick_key, (seq_total, image_slots), 0, 2)
    small_row = jax.random.randint(row_key, (), 0, seq_total)
    row_index = jnp.arange(seq_total, dtype=jnp.int32)
    picks = jnp.where(row_index[:, None] == small_row, 0, picks)
    sizes = jnp.where(picks == 1, IMG_B, IMG_A).astype(jnp.int32)
    ends = jnp.cumsum(sizes, axis=1)
    places = jnp.arange(SEQ, dtype=jnp.int32)
    ended = ends[:, None, :] <= places[None, :, None]
    ident = jnp.sum(ended.astype(jnp.int32), axis=2)
    last_end = jnp.max(jnp.where(ends <= SEQ, ends, 0), axis=1)
    labels = jnp.where(places[None, :] < last_end[:, None], ident, -1)
    return labels.reshape(TOKENS).astype(jnp.int32)


def draw_priority(key, part):
    key = jax.random.fold_in(key, 11)
    keys = jax.random.split(key, GROUPS)
    orders = jax.vmap(lambda single: jax.random.permutation(single, GROUP_TOK))(keys).reshape(TOKENS).astype(jnp.int32)
    levels = (TOP - 1 - jnp.arange(TOP, dtype=jnp.int32)) * GROUP_TOK
    return (levels[None, :] + orders[:, None]).astype(jnp.int32)


def block_levels(stream_key, dims, shards, smallest, largest):
    def one(position, parts):
        steps = jax.random.uniform(jax.random.fold_in(jax.random.fold_in(stream_key, 6), position), (parts,), jnp.float32, smallest / len(shards), largest / len(shards))
        return jnp.repeat(jnp.exp(steps), dims[position] // parts).reshape((-1,) + (1,) * (len(dims) - position - 1))

    loudness = one(*shards[0])
    for cut in shards[1:]:
        loudness = loudness * one(*cut)
    return loudness


def assign_block(key, own, number, rows, count, top, most, lean):
    order = jax.random.permutation(key, count)
    crowded, ordinary = shares(count, rows * top, most, lean, True), shares(count, rows * top, most, lean, False)
    places = jnp.arange(count)

    def named(sizes, offset_by):
        used = int((sizes > 0).sum())
        fixed = max(1, used // 4)
        moved = fixed + (places - fixed + offset_by * (used - fixed)) % max(1, count - fixed)
        return jnp.zeros((count,), jnp.int32).at[order[jnp.where(places < fixed, places, moved)]].set(jnp.asarray(sizes, jnp.int32))

    sizes = jnp.where(number % 4 == 0, named(crowded, number // 4), named(ordinary, number - number // 4 - 1))
    mixed = jax.random.permutation(jax.random.fold_in(own, 3), count)
    source_of, receiver = mixed[0:count // 2 * 2:2], mixed[1:count // 2 * 2:2]
    slack = jnp.minimum(sizes[source_of] - 1, most - sizes[receiver]) // 2
    slack = jnp.where((source_of == order[0]) | (receiver == order[0]) | (sizes[receiver] == 0), 0, jnp.maximum(slack, 0))
    moved = jax.random.randint(jax.random.fold_in(own, 4), (count // 2,), 0, 1 << 20) % (slack + 1)
    sizes = sizes.at[source_of].add(-moved).at[receiver].add(moved)
    items = jnp.searchsorted(jnp.cumsum(sizes), jnp.arange(rows * top), side="right").astype(jnp.int32)
    table = items.reshape(top, rows).T
    table = table[jax.random.permutation(jax.random.fold_in(own, 1), rows)]
    offset_by = jax.random.randint(jax.random.fold_in(own, 2), (rows, 1), 0, top)
    return jnp.take_along_axis(table, (jnp.arange(top)[None, :] + offset_by) % top, axis=1)


def shares(count, total, limit, slope, full):
    loads = [(1 << 20) // math.isqrt(standing ** slope) + 1 for standing in range(1, count + 1)]
    largest = limit if full else min(limit, max(-(-total // count), total * loads[0] // sum(loads)))
    least = 1 if total - largest >= count - 1 else 0
    holding, rest = [largest] + [least] * (count - 1), total - largest - least * (count - 1)
    while rest > 0:
        candidates = [i for i in range(1, count) if holding[i] < largest] or [i for i in range(1, count) if holding[i] < limit]
        mass, remaining = sum([loads[i] for i in candidates]), rest
        for i in candidates:
            addition = min(limit - holding[i], max(1, remaining * loads[i] // mass), rest)
            holding[i] = holding[i] + addition
            rest = rest - addition
    return np.array(holding)


def bell_draw(stream_key, dims, width, reach, pieces=(), held_as=jnp.bfloat16):
    values = width * jax.random.normal(stream_key, dims, jnp.float32)
    if pieces:
        values = values * block_levels(stream_key, dims, pieces, -0.22, 0.18)
    return jnp.clip(values, -reach, reach).astype(held_as)


def setup_inputs(seed: int = 0) -> dict:
    arg_keys = jax.random.split(jax.random.key(seed), 19)
    tokens = bell_draw(arg_keys[0], (TOKENS, D), 1.0, 6.0, ((0, 32),))
    segments = draw_segments(jax.random.fold_in(arg_keys[18], 71), 0)
    experts_keys = jax.random.split(jax.random.fold_in(arg_keys[2], 1), TOKENS // TOK_DEV)
    experts_turns = jax.random.permutation(jax.random.fold_in(arg_keys[2], 3), TOKENS // TOK_DEV)
    experts = jax.vmap(lambda own, number: assign_block(jax.random.fold_in(arg_keys[2], 2), own, number, TOK_DEV, E, TOP, MOST, 1))(experts_keys, experts_turns).reshape((TOKENS, TOP))
    priority = draw_priority(jax.random.fold_in(arg_keys[18], 71), 0)
    cotangent = bell_draw(arg_keys[4], (TOKENS, D), 1.0, 6.0, ((0, 32),))
    ln1_gain = jnp.clip(1.0 + 0.1 * jax.random.normal(arg_keys[5], (D,), jnp.float32), 0.5, 1.5)
    ln1_bias = bell_draw(arg_keys[6], (D,), 0.2, 1.0, (), jnp.float32)
    w_qkv = bell_draw(arg_keys[7], (D, 3 * D), D ** -0.5, 0.25)
    w_attn_out = bell_draw(arg_keys[8], (D, D), (max(D // 64, 1)) ** -0.5, 2.0)
    ln2_gain = jnp.clip(1.0 + 0.1 * jax.random.normal(arg_keys[9], (D,), jnp.float32), 0.5, 1.5)
    ln2_bias = bell_draw(arg_keys[10], (D,), 0.2, 1.0, (), jnp.float32)
    w_up = bell_draw(arg_keys[11], (D, FF), D ** -0.5, 0.25)
    w_down = bell_draw(arg_keys[12], (FF, D), FF ** -0.5, 0.125)
    ln3_gain = jnp.clip(1.0 + 0.1 * jax.random.normal(arg_keys[13], (D,), jnp.float32), 0.5, 1.5)
    ln3_bias = bell_draw(arg_keys[14], (D,), 0.2, 1.0, (), jnp.float32)
    w_router = bell_draw(arg_keys[15], (D, E), (2 * D) ** -0.5, 0.1875)
    expert_up = bell_draw(arg_keys[16], (E, D, FF), D ** -0.5, 0.25, ((0, 4),))
    expert_down = bell_draw(arg_keys[17], (E, FF, D), (max(FF // (16 * E), 1)) ** -0.5, 1.5, ((0, 4),))
    return {"tokens": tokens, "segments": segments, "experts": experts, "priority": priority, "cotangent": cotangent, "ln1_gain": ln1_gain, "ln1_bias": ln1_bias, "w_qkv": w_qkv, "w_attn_out": w_attn_out, "ln2_gain": ln2_gain, "ln2_bias": ln2_bias, "w_up": w_up, "w_down": w_down, "ln3_gain": ln3_gain, "ln3_bias": ln3_bias, "w_router": w_router, "expert_up": expert_up, "expert_down": expert_down}


epsilon = 1e-06
score_scale = 0.125
masked_score = -1e+30
highest = lax.Precision.HIGHEST

@jax.custom_vjp
def low(v):
    return lax.optimization_barrier(v.astype(jnp.bfloat16)).astype(jnp.float32)

@jax.custom_vjp
def low_back(v):
    return v

def low_keep(v):
    return (low(v), None)

def low_pass(kept, grad):
    return (grad,)

def back_keep(v):
    return (v, None)

def back_low(kept, grad):
    return (low(grad),)
low.defvjp(low_keep, low_pass)
low_back.defvjp(back_keep, back_low)

def norm_apply(values, norm_gain, norm_shift):
    centre = values - lax.optimization_barrier(jnp.mean(values, axis=-1, keepdims=True))
    inverse = lax.rsqrt(lax.optimization_barrier(jnp.mean(centre * centre, axis=-1, keepdims=True)) + epsilon)
    return centre * inverse * norm_gain + norm_shift

def gelu_tanh(values):
    return jax.nn.gelu(values, approximate=True)

def attention(u_low, seg_ids, weight_qkv, weight_out):
    qkv = jnp.dot(u_low, weight_qkv, precision=highest).reshape(SEQ, 3, HEADS, HD)
    queries = low_back(low(qkv[:, 0]))
    key_rows = low_back(low(qkv[:, 1]))
    value_rows = low_back(low(qkv[:, 2]))
    scores = jnp.einsum('qhd,khd->hqk', queries, key_rows, precision=highest) * score_scale
    scores = low_back(scores)
    same_image = seg_ids[:, None] == seg_ids[None, :]
    scores = jnp.where(same_image[None], scores, masked_score)
    row_peak = lax.optimization_barrier(jnp.max(scores, axis=2, keepdims=True))
    exp_scores = jnp.exp(scores - row_peak)
    attn_probs = exp_scores / lax.optimization_barrier(jnp.sum(exp_scores, axis=2, keepdims=True))
    mixed = jnp.einsum('hqk,khd->qhd', low(attn_probs), value_rows, precision=highest).reshape(SEQ, D)
    mixed = low_back(low(mixed))
    return low_back(jnp.dot(mixed, weight_out, precision=highest))

def dense_sequence(params, values, seg_ids):
    u1 = low(norm_apply(values, params['ln1_gain'], params['ln1_bias']))
    x1 = values + attention(u1, seg_ids, params['w_qkv'], params['w_attn_out'])
    u2 = low(norm_apply(x1, params['ln2_gain'], params['ln2_bias']))
    hidden = low_back(jnp.dot(u2, params['w_up'], precision=highest))
    active = low(gelu_tanh(hidden))
    return x1 + low_back(jnp.dot(active, params['w_down'], precision=highest))

def cutoff_mask(choice_ids, ranks):
    flat_ids = choice_ids.reshape(-1)
    flat_ranks = ranks.reshape(-1)
    labels = jnp.arange(E, dtype=jnp.int32)
    table = jnp.where(flat_ids[None, :] == labels[:, None], flat_ranks[None, :], -1)
    bound = lax.top_k(table, CAP)[0][:, CAP - 1]
    return flat_ranks >= bound[flat_ids]

def expert_rows(weight_up, weight_down, inputs):
    hidden = low_back(jnp.dot(inputs, weight_up, precision=highest))
    active = low(gelu_tanh(hidden))
    return low_back(low(jnp.dot(active, weight_down, precision=highest)))

def moe_group(params, x2, choice_ids, ranks):
    u3 = low(norm_apply(x2, params['ln3_gain'], params['ln3_bias']))
    logits = low_back(jnp.dot(u3, params['w_router'], precision=highest))
    gates = jax.nn.softmax(logits, axis=1)
    flat_ids = choice_ids.reshape(-1)
    kept_mask = cutoff_mask(choice_ids, ranks)
    pick_count = flat_ids.shape[0]
    labels = jnp.arange(E, dtype=jnp.int32)
    chosen = (flat_ids[None, :] == labels[:, None]) & kept_mask[None, :]
    places = jnp.cumsum(chosen.astype(jnp.int32), axis=1) - 1
    places = jnp.where(chosen, places, CAP)
    filler = jnp.arange(pick_count, dtype=jnp.int32)
    owner_rows = jax.vmap(lambda spots: jnp.full((CAP,), pick_count, jnp.int32).at[spots].set(filler, mode='drop'))(places)
    padded = jnp.concatenate([u3, jnp.zeros((1, D), jnp.float32)], axis=0)
    inputs = low_back(padded[owner_rows // TOP])
    outputs = lax.map(lambda pack: jax.checkpoint(expert_rows)(pack[0], pack[1], pack[2]), (params['expert_up'], params['expert_down'], inputs))
    spread = jnp.zeros((pick_count + 1, D), jnp.float32).at[owner_rows.reshape(-1)].set(outputs.reshape(-1, D))
    per_choice = spread[:pick_count].reshape(-1, TOP, D)
    gate_pick = jnp.take_along_axis(gates, choice_ids, axis=1)
    return x2 + lax.optimization_barrier(jnp.sum(gate_pick[:, :, None] * per_choice, axis=1))

def group_forward(params, values, seg_ids, choice_ids, ranks):
    seqs = values.reshape(-1, SEQ, D)
    seg_rows = seg_ids.reshape(-1, SEQ)
    dense_out = lax.map(lambda pack: jax.checkpoint(dense_sequence)(params, pack[0], pack[1]), (seqs, seg_rows))
    return moe_group(params, dense_out.reshape(GROUP_TOK, D), choice_ids, ranks)

def group_counts(choice_ids, ranks):
    kept_mask = cutoff_mask(choice_ids, ranks)
    hits = choice_ids.reshape(-1)[:, None] == jnp.arange(E, dtype=jnp.int32)[None, :]
    kept_total = lax.optimization_barrier(jnp.sum(hits & kept_mask[:, None], axis=0)).astype(jnp.float32)
    routed = lax.optimization_barrier(jnp.sum(hits, axis=0)).astype(jnp.float32)
    return jnp.stack([kept_total, routed - kept_total], axis=1)

def reference(tokens, segments, experts, priority, cotangent, ln1_gain, ln1_bias, w_qkv, w_attn_out, ln2_gain, ln2_bias, w_up, w_down, ln3_gain, ln3_bias, w_router, expert_up, expert_down):
    names = ('ln1_gain', 'ln1_bias', 'w_qkv', 'w_attn_out', 'ln2_gain', 'ln2_bias', 'w_up', 'w_down', 'ln3_gain', 'ln3_bias', 'w_router', 'expert_up', 'expert_down')
    arrays = (ln1_gain, ln1_bias, w_qkv, w_attn_out, ln2_gain, ln2_bias, w_up, w_down, ln3_gain, ln3_bias, w_router, expert_up, expert_down)
    params = {name: array.astype(jnp.float32) for name, array in zip(names, arrays)}
    seg_groups = segments.reshape(GROUPS, GROUP_TOK)
    id_groups = experts.reshape(GROUPS, GROUP_TOK, TOP)
    rank_groups = priority.reshape(GROUPS, GROUP_TOK, TOP)

    def forward(weights, values):
        blocks = values.reshape(GROUPS, GROUP_TOK, D)
        result = lax.map(lambda pack: jax.checkpoint(group_forward)(weights, pack[0], pack[1], pack[2], pack[3]), (blocks, seg_groups, id_groups, rank_groups))
        return result.reshape(TOKENS, D)
    final, pull = jax.vjp(forward, params, tokens.astype(jnp.float32))
    grads, grad_tokens = pull(cotangent.astype(jnp.float32))
    counts = lax.optimization_barrier(jnp.sum(lax.map(lambda pack: group_counts(pack[0], pack[1]), (id_groups, rank_groups)), axis=0))
    return (final.astype(jnp.bfloat16), grad_tokens, grads['ln1_gain'], grads['ln1_bias'], grads['w_qkv'], grads['w_attn_out'], grads['ln2_gain'], grads['ln2_bias'], grads['w_up'], grads['w_down'], grads['ln3_gain'], grads['ln3_bias'], grads['w_router'], grads['expert_up'], grads['expert_down'], counts)
```

```python
import functools
import math

import jax
import jax.numpy as jnp
from jax import lax
from jax.experimental import pallas as pl
from jax.experimental.pallas import tpu as pltpu
from jax.sharding import PartitionSpec as P

MESH = pl.DeviceIdType.MESH
F32 = jnp.float32
BF16 = jnp.bfloat16
HD = 64
DP = "dp"
EXPERT = "expert"
VMEM_PLAN = 57 << 20
PAIR = 2 * HD
epsilon = 1e-06
GELU_C = 0.7978845608028654
GELU_A = 0.044715


HEADS = 8
TOP = 2
SEQ = 512
score_scale = 0.125
masked_score = -1e30


def norm_forward(values, norm_gain, norm_shift):
    centre = values - jnp.mean(values, axis=1, keepdims=True)
    inverse = lax.rsqrt(jnp.mean(centre * centre, axis=1, keepdims=True) + epsilon)
    normed = centre * inverse
    return (normed * norm_gain + norm_shift, normed, inverse)


def norm_backward(upstream, normed, inverse, norm_gain):
    scaled = upstream * norm_gain
    inner = (
        scaled
        - jnp.mean(scaled, axis=1, keepdims=True)
        - normed * jnp.mean(scaled * normed, axis=1, keepdims=True)
    )
    return (inverse * inner, jnp.sum(upstream * normed, axis=0), jnp.sum(upstream, axis=0))


def gelu_tanh(values):
    return jax.nn.gelu(values, approximate=True)


def gelu_pull(values, upstream):
    return jax.vjp(gelu_tanh, values)[1](upstream)[0]


def masked_scores(query_rows, key_rows, query_seg, key_seg):
    raw_scores = (
        jnp.einsum("qhd,khd->hqk", query_rows, key_rows, preferred_element_type=jnp.float32)
        * score_scale
    )
    same_image = query_seg[:, None] == key_seg[None, :]
    return jnp.where(same_image[None], raw_scores, masked_score)


def attend_forward(queries, key_rows, value_rows, seg_ids):
    outputs, log_sums = ([], [])
    scores = masked_scores(queries, key_rows, seg_ids, seg_ids)
    row_peak = jnp.max(scores, axis=2, keepdims=True)
    exp_scores = jnp.exp(scores - row_peak)
    row_total = jnp.sum(exp_scores, axis=2, keepdims=True)
    attn_probs = (exp_scores / row_total).astype(jnp.bfloat16)
    outputs.append(
        jnp.einsum("hqk,khd->qhd", attn_probs, value_rows, preferred_element_type=jnp.float32)
    )
    log_sums.append(row_peak + jnp.log(row_total))
    return (outputs[0], log_sums[0])


def attend_backward(queries, key_rows, value_rows, seg_ids, log_sums, upstream):
    scores = masked_scores(queries, key_rows, seg_ids, seg_ids)
    attn_probs = jnp.exp(scores - log_sums)
    grad_values = jnp.einsum(
        "hqk,qhd->khd",
        attn_probs.astype(jnp.bfloat16),
        upstream,
        preferred_element_type=jnp.float32,
    )
    grad_probs = jnp.einsum(
        "qhd,khd->hqk", upstream, value_rows, preferred_element_type=jnp.float32
    )
    centred = grad_probs - jnp.sum(attn_probs * grad_probs, axis=2, keepdims=True)
    grad_scores = (attn_probs * centred).astype(jnp.bfloat16)
    grad_queries = (
        jnp.einsum("hqk,khd->qhd", grad_scores, key_rows, preferred_element_type=jnp.float32)
        * score_scale
    )
    grad_keys = (
        jnp.einsum("hqk,qhd->khd", grad_scores, queries, preferred_element_type=jnp.float32)
        * score_scale
    )
    return (grad_queries, grad_keys, grad_values)


def pick_rows(table, index_rows):
    return table[index_rows]


def plain_shards(
    tokens,
    segments,
    experts,
    priority,
    cotangent,
    ln1_gain,
    ln1_bias,
    w_qkv,
    w_attn_out,
    ln2_gain,
    ln2_bias,
    w_up,
    w_down,
    ln3_gain,
    ln3_bias,
    w_router,
    expert_up,
    expert_down,
):
    row_count, width = tokens.shape
    seq_count = row_count // SEQ
    expert_total = w_router.shape[1]
    local_experts = expert_up.shape[0]
    owner_count = lax.axis_size(EXPERT)
    slot_depth = 3 * row_count // expert_total
    capacity = (21 * row_count + 10 * local_experts - 1) // (10 * local_experts)
    arrive_rows = owner_count * slot_depth
    buffer_rows = local_experts * arrive_rows
    pick_count = row_count * TOP
    rank_span = pick_count * owner_count
    labels = jnp.arange(expert_total, dtype=jnp.int32)
    x_in = tokens.astype(jnp.float32)
    u1, normed1, inverse1 = norm_forward(x_in, ln1_gain, ln1_bias)
    u1_low = u1.astype(jnp.bfloat16)
    qkv_low = jnp.dot(u1_low, w_qkv, preferred_element_type=jnp.float32).astype(jnp.bfloat16)
    qkv_seq = qkv_low.reshape(seq_count, SEQ, 3, HEADS, HD)
    seg_seq = segments.reshape(seq_count, SEQ)
    mixed_parts, lse_parts = ([], [])
    seq_index = 0
    mixed_one, lse_one = attend_forward(
        qkv_seq[seq_index, :, 0],
        qkv_seq[seq_index, :, 1],
        qkv_seq[seq_index, :, 2],
        seg_seq[seq_index],
    )
    mixed_parts.append(mixed_one)
    lse_parts.append(lse_one)
    mixed_low = mixed_parts[0].reshape(row_count, width).astype(jnp.bfloat16)
    x1 = x_in + jnp.dot(mixed_low, w_attn_out, preferred_element_type=jnp.float32)
    u2, normed2, inverse2 = norm_forward(x1, ln2_gain, ln2_bias)
    u2_low = u2.astype(jnp.bfloat16)
    hidden2 = jnp.dot(u2_low, w_up, preferred_element_type=jnp.float32)
    active2 = gelu_tanh(hidden2).astype(jnp.bfloat16)
    x2 = x1 + jnp.dot(active2, w_down, preferred_element_type=jnp.float32)
    u3, normed3, inverse3 = norm_forward(x2, ln3_gain, ln3_bias)
    u3_low = u3.astype(jnp.bfloat16)
    logits = jnp.dot(u3_low, w_router, preferred_element_type=jnp.float32)
    exp_logits = jnp.exp(logits - jnp.max(logits, axis=1, keepdims=True))
    gates = exp_logits / jnp.sum(exp_logits, axis=1, keepdims=True)
    flat_ids = experts.reshape(-1)
    flat_ranks = priority.reshape(-1)
    hits = flat_ids[:, None] == labels[None, :]
    all_ids, all_ranks = (
        lax.all_gather(experts, EXPERT, axis=0, tiled=True),
        lax.all_gather(priority, EXPERT, axis=0, tiled=True),
    )
    id_at_rank = (
        jnp.zeros((rank_span,), jnp.int32).at[all_ranks.reshape(-1)].set(all_ids.reshape(-1))
    )
    marks = (id_at_rank[:, None] == labels[None, :]).astype(jnp.int32)
    above = jnp.cumsum(marks[::-1], axis=0)[::-1]
    kept_mask = above[flat_ranks, flat_ids] <= capacity
    chosen = hits & kept_mask[:, None]
    running = jnp.cumsum(chosen.astype(jnp.int32), axis=0) - 1
    slot_of = jnp.sum(jnp.where(chosen, running, 0), axis=1)
    target = (
        flat_ids % local_experts * arrive_rows + flat_ids // local_experts * slot_depth + slot_of
    )
    target = jnp.where(kept_mask, target, buffer_rows)
    source_pick = (
        jnp.full((buffer_rows,), pick_count, jnp.int32)
        .at[target]
        .set(jnp.arange(pick_count, dtype=jnp.int32), mode="drop")
    )
    send_flags = (
        (source_pick < pick_count)
        .astype(jnp.bfloat16)
        .reshape(local_experts, owner_count, slot_depth)
    )
    u3_pad = jnp.concatenate([u3_low, jnp.zeros((1, width), jnp.bfloat16)], axis=0)
    send_rows = u3_pad[source_pick // TOP].reshape(local_experts, owner_count, slot_depth, width)
    kept_total = jnp.sum(chosen, axis=0).astype(jnp.float32)
    routed = jnp.sum(hits, axis=0).astype(jnp.float32)
    counts = jnp.stack([kept_total, routed - kept_total], axis=1)
    recv_rows, recv_flags = (
        lax.all_to_all(send_rows, EXPERT, split_axis=1, concat_axis=1, tiled=True),
        lax.all_to_all(send_flags, EXPERT, split_axis=1, concat_axis=1, tiled=True),
    )
    recv_rows = recv_rows.reshape(local_experts, arrive_rows, width)
    valid = recv_flags.reshape(local_experts, arrive_rows) > 0
    places = jnp.cumsum(valid.astype(jnp.int32), axis=1) - 1
    places = jnp.where(valid, places, capacity)
    filler = jnp.arange(arrive_rows, dtype=jnp.int32)
    gather_index = jax.vmap(
        lambda spots: jnp.full((capacity,), arrive_rows, jnp.int32)
        .at[spots]
        .set(filler, mode="drop")
    )(places)
    zero_row = jnp.zeros((local_experts, 1, width), jnp.bfloat16)
    expert_in = jax.vmap(pick_rows)(jnp.concatenate([recv_rows, zero_row], axis=1), gather_index)
    expert_hidden = jnp.einsum(
        "ecd,edf->ecf", expert_in, expert_up, preferred_element_type=jnp.float32
    )
    expert_act = gelu_tanh(expert_hidden).astype(jnp.bfloat16)
    expert_out = jnp.einsum(
        "ecf,efd->ecd", expert_act, expert_down, preferred_element_type=jnp.float32
    ).astype(jnp.bfloat16)
    back_rows = jax.vmap(pick_rows)(jnp.concatenate([expert_out, zero_row], axis=1), places)
    returned = lax.all_to_all(
        back_rows.reshape(local_experts, owner_count, slot_depth, width),
        EXPERT,
        split_axis=1,
        concat_axis=1,
        tiled=True,
    )
    returned_pad = jnp.concatenate(
        [returned.reshape(buffer_rows, width), jnp.zeros((1, width), jnp.bfloat16)], axis=0
    )
    y_pair = returned_pad[target].reshape(row_count, TOP, width).astype(jnp.float32)
    pair_hit = experts[:, :, None] == labels[None, None, :]
    gate_pick = jnp.sum(jnp.where(pair_hit, gates[:, None, :], 0.0), axis=2)
    x3 = x2 + jnp.sum(gate_pick[:, :, None] * y_pair, axis=1)
    output = x3.astype(jnp.bfloat16)
    grad_out = cotangent.astype(jnp.float32)
    grad_y = (
        (gate_pick[:, :, None] * grad_out[:, None, :])
        .reshape(pick_count, width)
        .astype(jnp.bfloat16)
    )
    grad_y_pad = jnp.concatenate([grad_y, jnp.zeros((1, width), jnp.bfloat16)], axis=0)
    grad_send = grad_y_pad[source_pick].reshape(local_experts, owner_count, slot_depth, width)
    grad_recv = lax.all_to_all(
        grad_send, EXPERT, split_axis=1, concat_axis=1, tiled=True
    ).reshape(local_experts, arrive_rows, width)
    grad_expert_y = jax.vmap(pick_rows)(
        jnp.concatenate([grad_recv, zero_row], axis=1), gather_index
    )
    grad_expert_down = jnp.einsum(
        "ecf,ecd->efd", expert_act, grad_expert_y, preferred_element_type=jnp.float32
    )
    grad_expert_act = jnp.einsum(
        "ecd,efd->ecf", grad_expert_y, expert_down, preferred_element_type=jnp.float32
    )
    grad_expert_hidden = gelu_pull(expert_hidden, grad_expert_act).astype(jnp.bfloat16)
    grad_expert_up = jnp.einsum(
        "ecd,ecf->edf", expert_in, grad_expert_hidden, preferred_element_type=jnp.float32
    )
    grad_expert_in = jnp.einsum(
        "ecf,edf->ecd", grad_expert_hidden, expert_up, preferred_element_type=jnp.float32
    ).astype(jnp.bfloat16)
    grad_back = jax.vmap(pick_rows)(jnp.concatenate([grad_expert_in, zero_row], axis=1), places)
    grad_home = lax.all_to_all(
        grad_back.reshape(local_experts, owner_count, slot_depth, width),
        EXPERT,
        split_axis=1,
        concat_axis=1,
        tiled=True,
    )
    grad_home_pad = jnp.concatenate(
        [grad_home.reshape(buffer_rows, width), jnp.zeros((1, width), jnp.bfloat16)], axis=0
    )
    grad_u3 = jnp.sum(
        grad_home_pad[target].reshape(row_count, TOP, width).astype(jnp.float32), axis=1
    )
    expert_shares = (
        lax.psum_scatter(
            grad_expert_up.astype(jnp.bfloat16), DP, scatter_dimension=1, tiled=True
        ).astype(jnp.float32),
        lax.psum_scatter(
            grad_expert_down.astype(jnp.bfloat16), DP, scatter_dimension=1, tiled=True
        ).astype(jnp.float32),
    )
    grad_pick = jnp.sum(grad_out[:, None, :] * y_pair, axis=2)
    grad_gates = jnp.sum(jnp.where(pair_hit, grad_pick[:, :, None], 0.0), axis=1)
    grad_logits = (
        gates * (grad_gates - jnp.sum(gates * grad_gates, axis=1, keepdims=True))
    ).astype(jnp.bfloat16)
    grad_router = jnp.einsum("rd,re->de", u3_low, grad_logits, preferred_element_type=jnp.float32)
    grad_u3 = grad_u3 + jnp.einsum(
        "re,de->rd", grad_logits, w_router, preferred_element_type=jnp.float32
    )
    grad_x2_norm, grad_ln3_gain, grad_ln3_bias = norm_backward(grad_u3, normed3, inverse3, ln3_gain)
    grad_x2 = grad_out + grad_x2_norm
    grad_m = grad_x2.astype(jnp.bfloat16)
    grad_down = jnp.einsum("rf,rd->fd", active2, grad_m, preferred_element_type=jnp.float32)
    grad_active2 = jnp.einsum("rd,fd->rf", grad_m, w_down, preferred_element_type=jnp.float32)
    grad_hidden2 = gelu_pull(hidden2, grad_active2).astype(jnp.bfloat16)
    grad_up = jnp.einsum("rd,rf->df", u2_low, grad_hidden2, preferred_element_type=jnp.float32)
    grad_u2 = jnp.einsum("rf,df->rd", grad_hidden2, w_up, preferred_element_type=jnp.float32)
    grad_x1_norm, grad_ln2_gain, grad_ln2_bias = norm_backward(grad_u2, normed2, inverse2, ln2_gain)
    grad_x1 = grad_x2 + grad_x1_norm
    grad_o = grad_x1.astype(jnp.bfloat16)
    grad_attn_out = jnp.einsum("rd,re->de", mixed_low, grad_o, preferred_element_type=jnp.float32)
    grad_mixed = jnp.einsum(
        "re,de->rd", grad_o, w_attn_out, preferred_element_type=jnp.float32
    ).astype(jnp.bfloat16)
    grad_mixed_seq = grad_mixed.reshape(seq_count, SEQ, HEADS, HD)
    seq_index = 0
    grad_q, grad_k, grad_v = attend_backward(
        qkv_seq[seq_index, :, 0],
        qkv_seq[seq_index, :, 1],
        qkv_seq[seq_index, :, 2],
        seg_seq[seq_index],
        lse_parts[seq_index],
        grad_mixed_seq[seq_index],
    )
    grad_parts = jnp.stack([grad_q, grad_k, grad_v], axis=1)
    grad_qkv_low = grad_parts.reshape(row_count, 3 * width).astype(jnp.bfloat16)
    grad_qkv = jnp.einsum("rd,re->de", u1_low, grad_qkv_low, preferred_element_type=jnp.float32)
    grad_u1 = jnp.einsum("re,de->rd", grad_qkv_low, w_qkv, preferred_element_type=jnp.float32)
    grad_x0_norm, grad_ln1_gain, grad_ln1_bias = norm_backward(grad_u1, normed1, inverse1, ln1_gain)
    grad_tokens = grad_x1 + grad_x0_norm
    dense_parts = (
        lax.psum_scatter(
            grad_qkv.astype(jnp.bfloat16), EXPERT, scatter_dimension=0, tiled=True
        ).astype(jnp.float32),
        lax.psum_scatter(
            grad_attn_out.astype(jnp.bfloat16), EXPERT, scatter_dimension=0, tiled=True
        ).astype(jnp.float32),
        lax.psum_scatter(
            grad_up.astype(jnp.bfloat16), EXPERT, scatter_dimension=0, tiled=True
        ).astype(jnp.float32),
        lax.psum_scatter(
            grad_down.astype(jnp.bfloat16), EXPERT, scatter_dimension=0, tiled=True
        ).astype(jnp.float32),
        lax.psum_scatter(
            grad_router.astype(jnp.bfloat16), EXPERT, scatter_dimension=0, tiled=True
        ).astype(jnp.float32),
        lax.psum_scatter(
            grad_ln1_gain.astype(jnp.bfloat16), EXPERT, scatter_dimension=0, tiled=True
        ).astype(jnp.float32),
        lax.psum_scatter(
            grad_ln1_bias.astype(jnp.bfloat16), EXPERT, scatter_dimension=0, tiled=True
        ).astype(jnp.float32),
        lax.psum_scatter(
            grad_ln2_gain.astype(jnp.bfloat16), EXPERT, scatter_dimension=0, tiled=True
        ).astype(jnp.float32),
        lax.psum_scatter(
            grad_ln2_bias.astype(jnp.bfloat16), EXPERT, scatter_dimension=0, tiled=True
        ).astype(jnp.float32),
        lax.psum_scatter(
            grad_ln3_gain.astype(jnp.bfloat16), EXPERT, scatter_dimension=0, tiled=True
        ).astype(jnp.float32),
        lax.psum_scatter(
            grad_ln3_bias.astype(jnp.bfloat16), EXPERT, scatter_dimension=0, tiled=True
        ).astype(jnp.float32),
        lax.psum_scatter(
            counts.astype(jnp.bfloat16), EXPERT, scatter_dimension=0, tiled=True
        ).astype(jnp.float32),
    )
    dense_sums = (
        lax.psum(dense_parts[0].astype(jnp.bfloat16), DP).astype(jnp.float32),
        lax.psum(dense_parts[1].astype(jnp.bfloat16), DP).astype(jnp.float32),
        lax.psum(dense_parts[2].astype(jnp.bfloat16), DP).astype(jnp.float32),
        lax.psum(dense_parts[3].astype(jnp.bfloat16), DP).astype(jnp.float32),
        lax.psum(dense_parts[4].astype(jnp.bfloat16), DP).astype(jnp.float32),
        lax.psum(dense_parts[5].astype(jnp.bfloat16), DP).astype(jnp.float32),
        lax.psum(dense_parts[6].astype(jnp.bfloat16), DP).astype(jnp.float32),
        lax.psum(dense_parts[7].astype(jnp.bfloat16), DP).astype(jnp.float32),
        lax.psum(dense_parts[8].astype(jnp.bfloat16), DP).astype(jnp.float32),
        lax.psum(dense_parts[9].astype(jnp.bfloat16), DP).astype(jnp.float32),
        lax.psum(dense_parts[10].astype(jnp.bfloat16), DP).astype(jnp.float32),
        lax.psum(dense_parts[11].astype(jnp.bfloat16), DP).astype(jnp.float32),
    )
    (
        sum_qkv,
        sum_attn_out,
        sum_up,
        sum_down,
        sum_router,
        sum_g1,
        sum_b1,
        sum_g2,
        sum_b2,
        sum_g3,
        sum_b3,
        sum_counts,
    ) = dense_sums
    share_up, share_down = expert_shares
    return (
        output,
        grad_tokens,
        sum_g1,
        sum_b1,
        sum_qkv,
        sum_attn_out,
        sum_g2,
        sum_b2,
        sum_up,
        sum_down,
        sum_g3,
        sum_b3,
        sum_router,
        share_up,
        share_down,
        sum_counts,
    )


def mm(a, b):
    return lax.dot_general(a, b, (((1,), (0,)), ((), ())), preferred_element_type=F32)


def mm_nt(a, b):
    return lax.dot_general(a, b, (((1,), (1,)), ((), ())), preferred_element_type=F32)


def mm_tn(a, b):
    return lax.dot_general(a, b, (((0,), (0,)), ((), ())), preferred_element_type=F32)


def row_mean(v):
    return jnp.sum(v, axis=1, keepdims=True) * (1.0 / v.shape[1])


def norm_parts(v):
    centre = v - row_mean(v)
    inverse = lax.rsqrt(row_mean(centre * centre) + epsilon)
    return centre * inverse, inverse


def norm_back(v, du, gain):
    normed, inverse = norm_parts(v)
    dn = du * gain
    inner = dn - row_mean(dn) - normed * row_mean(dn * normed)
    return (
        inverse * inner,
        jnp.sum(du * normed, axis=0, keepdims=True),
        jnp.sum(du, axis=0, keepdims=True),
    )


def gelu_both(h):
    sq = h * h
    t = jnp.tanh(h * (GELU_C + GELU_C * GELU_A * sq))
    u = 0.5 + 0.5 * t
    act = h * u
    slope = u + act * (1.0 - t) * (GELU_C + 3.0 * GELU_C * GELU_A * sq)
    return act, slope


def tile(i, size):
    return pl.ds(pl.multiple_of(i * size, size), size)


NAMES_IN = ["tok", "cot", "ids", "ranks", "seg", "g1", "b1", "g2", "b2", "g3", "b3", "wr"]
NAMES_IN += ["wqkv_h", "wo_h", "wup_h", "wdn_h", "eup_h", "edn_h"]
NAMES_OUT = ["out", "gtok", "small", "gdn", "gup", "go", "gqkv", "geup", "gedn"]
DOWN, UP, ATTN, QKV = range(4)

START, TILE = 35.0, 2.3
FEED, STEP, LAG, HOP, WINDOW = 42.0, 5.8, 10.0, 7.0, 4
AFTER_EXPERTS, BEFORE_BACK, AFTER_NORM, AFTER_MLP = 57.0, 66.0, 75.0, 80.0
AFTER_MLP_GRADS, AFTER_OUT, PAIR_TIME = 84.0, 88.0, 2.5
LINE, LINE_HOP, SHARE_HOP = 104.0, 4.0, 3.0


class Named:
    def __init__(self, pairs):
        self.__dict__.update(pairs)


def make_kernel(
    rows, width, ff, local, experts_all, nx, ng, capacity, room, depth, scratch_names
):
    nz = ng // 2
    steps = nz
    ft = ff // steps
    half = rows // 2
    ep = max(16, experts_all)
    fb, wb = ff // ng, width // ng
    far_first = sorted(range(nz), key=lambda d: (-abs(2 * d - nz + 1), -d))

    def kernel(*refs):
        r = Named(zip(NAMES_IN + NAMES_OUT + scratch_names, refs))
        r.du = r.acc_a.at[pl.ds(0, rows), :]
        r.dx = r.acc_b.at[pl.ds(0, rows), :]
        r.low = r.dyr.at[pl.ds(0, rows), :]
        r.trans = r.xrt.at[:, pl.ds(0, rows)]
        me = lax.axis_index(EXPERT)
        dp = lax.axis_index(DP)
        z, core = dp // 2, lax.rem(dp, 2)
        mate = z * 2 + 1 - core

        across = me + 1 - 2 * lax.rem(me, 2)
        beside = lax.rem(me + 2, nx)

        def peer(k):
            return (me, across, beside, nx - 1 - me)[k]

        loads = [
            pltpu.make_async_copy(src, dst, r.load_sem.at[i])
            for i, (src, dst) in enumerate(
                (
                    (r.tok, r.tokv),
                    (r.wqkv_h, r.wqkv),
                    (r.wo_h, r.wo),
                    (r.wup_h, r.wup),
                    (r.wdn_h, r.wdn),
                    (r.eup_h, r.eup),
                    (r.edn_h, r.edn),
                )
            )
        ]
        loads[0].start()
        loads[1].start()
        own_dz = pltpu.make_async_copy(r.cot, r.dz, r.load_sem.at[7])
        own_dz.start()

        barrier = pltpu.get_barrier_semaphore()
        for k in range(1, nx):
            pl.semaphore_signal(
                barrier, inc=1, device_id={EXPERT: peer(k)}, device_id_type=MESH
            )
        for k in range(1, ng):
            pl.semaphore_signal(
                barrier, inc=1, device_id={DP: lax.rem(dp + k, ng)}, device_id_type=MESH
            )
        pl.semaphore_wait(barrier, nx - 1 + ng - 1)

        def to_expert(src, dst, send, receive, k):
            return pltpu.make_async_remote_copy(
                src_ref=src,
                dst_ref=dst,
                send_sem=send,
                recv_sem=receive,
                device_id={EXPERT: peer(k)},
                device_id_type=MESH,
            )

        def to_dp(src, dst, send, receive, target):
            return pltpu.make_async_remote_copy(
                src_ref=src,
                dst_ref=dst,
                send_sem=send,
                recv_sem=receive,
                device_id={DP: target},
                device_id_type=MESH,
            )

        def direct(src, dst, group, k):
            return to_expert(src, dst, r.send_sem.at[group, k], r.recv_sem.at[group, k], k)

        def rank_copy(k, slot):
            return direct(r.sp_out.at[peer(k)], r.sp_in.at[slot], 0, k)

        def gt_copy(k, slot):
            return direct(r.gt_out.at[peer(k)], r.gt_in.at[slot], 1, k)

        def row_copy(flow, l, k, slot):
            source, target = ((r.out_u, r.in_u), (r.out_z, r.in_z))[flow % 2]
            if flow >= 2:
                source, target = target, source
            at = (flow * local + l) * nx + k
            return to_expert(
                source.at[peer(k), l],
                target.at[slot, l],
                r.row_send.at[at],
                r.row_recv.at[at],
                k,
            )

        line_id = lax.broadcasted_iota(jnp.int32, (8 * nx, 1), 0)
        line_id = jnp.where(
            (line_id & 7) < local, (line_id >> 3) * local + (line_id & 7), -1
        )
        tab = jnp.full((8 * nx, rows), -1, jnp.int32)
        for k in range(r.ids.shape[0]):
            tab = jnp.where(r.ids[k : k + 1, :] == line_id, r.ranks[k : k + 1, :], tab)
        tab = tab.astype(F32)
        earlier = lax.broadcasted_iota(jnp.int32, (rows, rows), 0)
        earlier = jnp.where(earlier < lax.broadcasted_iota(jnp.int32, (rows, rows), 1), 1.0, 0.0)
        named = jnp.where(tab >= 0.0, 1.0, 0.0).astype(BF16)
        slots = jnp.where(tab >= 0.0, mm(named, earlier.astype(BF16)), -1.0)
        level = tab + 1.0
        high = jnp.floor(level * (1.0 / 128.0))
        low = level - 128.0 * high
        slot_id = lax.broadcasted_iota(jnp.int32, (depth, rows), 0).astype(F32)
        for j in range(nx):
            parts = jnp.concatenate(
                [high[8 * j : 8 * j + 8], low[8 * j : 8 * j + 8]], axis=0
            ).astype(BF16)
            r.sp_out[j] = jnp.full((8, depth), -1.0, F32)
            for l in range(local):
                at = 8 * j + l
                r.comp[j, l] = jnp.where(slot_id == slots[at : at + 1], 1.0, 0.0).astype(BF16)
                got = mm_nt(parts, r.comp[j, l])
                r.sp_out[j, l : l + 1, :] = 128.0 * got[l : l + 1] + got[8 + l : 9 + l] - 1.0
        for k in range(1, nx):
            rank_copy(k, me).start()
        r.sp_in[me] = r.sp_out[me]
        own_dz.wait()
        for l in range(local):
            for k in range(1, nx):
                r.out_z[peer(k), l] = mm(r.comp[peer(k), l], r.dz[...]).astype(BF16)
                if l == 0:
                    row_copy(1, l, k, me).start()
            r.in_z[me, l] = mm(r.comp[me, l], r.dz[...]).astype(BF16)
        for copy in loads[2:]:
            copy.start()

        def unit(kind, l, d):
            return (l * 2 + kind) * nz + d

        def block(kind, l, d, side):
            j = d * 2 + side
            if kind == DOWN:
                return r.edn.at[l, pl.ds(pl.multiple_of(j * fb, fb), fb), :]
            return r.eup.at[l, pl.ds(pl.multiple_of(j * wb, wb), wb), :]

        def mate_in(kind, l, d):
            if kind == DOWN:
                return r.xdn.at[l, pl.ds(d * fb, fb), :]
            return r.xup.at[l, pl.ds(d * wb, wb), :]

        def mate_copy(kind, l, d):
            u = unit(kind, l, d)
            return to_dp(
                block(kind, l, d, 1 - core),
                mate_in(kind, l, d),
                r.x_send.at[u],
                r.x_recv.at[u],
                mate,
            )

        def z_slot(kind, l, s):
            return (r.zdn if kind == DOWN else r.zup).at[l, s]

        def right_copy(kind, l, d):
            u = unit(kind, l, d)
            return to_dp(
                block(kind, l, d, core),
                z_slot(kind, l, d + 1),
                r.z_send.at[u],
                r.z_recv.at[u, 0],
                lax.rem(dp + 2, ng),
            )

        def left_copy(kind, l, d):
            u = unit(kind, l, d)
            return to_dp(
                block(kind, l, d, core),
                z_slot(kind, l, d),
                r.z_send.at[u],
                r.z_recv.at[u, 1],
                lax.rem(dp + ng - 2, ng),
            )

        def add_to(ref, other):
            ref[...] = (ref[...].astype(F32) + other[...].astype(F32)).astype(BF16)

        waiting, joined = [], set()

        def ready(m):
            return all(u in waiting or u in joined for u in (rightward[m], leftward[m]))

        def settle(m):
            while not {rightward[m], leftward[m]} <= joined:
                join(*waiting.pop(0))

        def join(kind, l, d):
            joined.add((kind, l, d))
            mate_copy(kind, l, d).wait_recv()
            add_to(block(kind, l, d, core), mate_in(kind, l, d))

        groups = [(kind, l) for l in range(local) for kind in (DOWN, UP)]
        rightward = [(kind, l, d) for kind, l in groups for d in reversed(range(1, nz))]
        leftward = [(kind, l, d) for kind, l in groups for d in range(nz - 1)]

        def feed(m):
            settle(m)

            @pl.when(z == 0)
            def _():
                if m >= WINDOW:
                    right_copy(*rightward[m - WINDOW]).wait_send()
                right_copy(*rightward[m]).start()

            @pl.when(z == nz - 1)
            def _():
                if m >= WINDOW:
                    left_copy(*leftward[m - WINDOW]).wait_send()
                left_copy(*leftward[m]).start()

        def hop(m, h):
            settle(m)
            right, left = rightward[m], leftward[m]
            if right[2] >= h:

                @pl.when(z == h)
                def _():
                    right_copy(*right).wait_recv()
                    add_to(block(*right, core), z_slot(*right[:2], right[2] + 1))
                    if right[2] > h:
                        right_copy(*right).start()

            if left[2] <= nz - 1 - h:

                @pl.when(z == nz - 1 - h)
                def _():
                    left_copy(*left).wait_recv()
                    add_to(block(*left, core), z_slot(*left))
                    if left[2] < nz - 1 - h:
                        left_copy(*left).start()

        shared = (
            (r.wdn, r.xdn, 0, r.bdn, r.cdn, ff, width),
            (r.wup, r.xup, 0, r.bup, r.cup, width, ff),
            (r.wo, r.xdn, 1, r.bo, r.co, width, width),
            (r.wqkv, r.xup, 1, r.bqkv, r.cqkv, width, 3 * width),
        )

        def sizes(t):
            q = shared[t][5] // nx
            return q, q // 2, q // 2 // nz

        def half_of(t, q, side):
            rq, rh, _ = sizes(t)
            return shared[t][0].at[pl.ds(pl.multiple_of(q * rq + side * rh, rh), rh), :]

        def part_of(t, d, side):
            rq, rh, rz = sizes(t)
            start = pl.multiple_of(me * rq + side * rh + d * rz, rz)
            return shared[t][0].at[pl.ds(start, rz), :]

        def swap_in(t, q):
            _, rh, _ = sizes(t)
            _, buffer, l, _, _, _, wide = shared[t]
            return buffer.at[l, pl.ds(pl.multiple_of(q * rh, rh), rh), pl.ds(0, wide)]

        def swap_copy(t, q):
            return to_dp(
                half_of(t, q, 1 - core),
                swap_in(t, q),
                r.a_send.at[t, q],
                r.a_recv.at[t, q],
                mate,
            )

        def quarter(t, k, c):
            rq, rh, _ = sizes(t)
            start = pl.multiple_of(peer(k) * rq + core * rh + c * (rh // 2), rh // 2)
            return shared[t][0].at[pl.ds(start, rh // 2), :]

        def plane_cross(t, c):
            return to_expert(
                quarter(t, 3, c),
                shared[t][3].at[2, c],
                r.b_send.at[t, 4 + c],
                r.b_recv.at[t, 4 + c],
                c + 1,
            )

        def plane_copy(t, k, c):
            at = (k - 1) * 2 + c
            return to_expert(
                quarter(t, k, c),
                shared[t][3].at[k - 1, c],
                r.b_send.at[t, at],
                r.b_recv.at[t, at],
                k,
            )

        def part_copy(t, d, step):
            return to_dp(
                part_of(t, d, core),
                shared[t][4].at[d + 1 if step > 0 else d],
                r.c_send.at[t, d],
                r.c_recv.at[t, d, 0 if step > 0 else 1],
                lax.rem(dp + ng + 2 * step, ng),
            )

        done = (
            r.s2.at[pl.ds(0, ff // nx), pl.ds(0, width)],
            r.a2.at[pl.ds(0, width // nx), :],
            r.s2.at[pl.ds(0, width // nx), pl.ds(width, width)],
            r.a2.at[pl.ds(width // nx, width // nx), pl.ds(0, 3 * width)],
        )

        def done_part(t, d, side):
            _, rh, rz = sizes(t)
            return done[t].at[pl.ds(pl.multiple_of(side * rh + d * rz, rz), rz), :]

        def share_copy(t, d, step):
            return to_dp(
                done_part(t, d, core),
                done_part(t, d, core),
                r.g_send.at[t, d, 0 if step > 0 else 1],
                r.g_recv.at[t, d],
                lax.rem(dp + ng + 2 * step, ng),
            )

        def give_copy(t, d, side):
            return to_dp(
                done_part(t, d, side),
                done_part(t, d, side),
                r.p_send.at[t, d],
                r.p_recv.at[t, d],
                mate,
            )

        def near_copy(t, k):
            return to_dp(
                part_of(t, lax.rem(z + k, nz), core),
                shared[t][4].at[k],
                r.c_send.at[t, k],
                r.c_recv.at[t, k, 0],
                lax.rem(dp + 2 * k, ng),
            )

        def all_copy(t, k, owner):
            part = done_part(t, owner // 2, lax.rem(owner, 2))
            send, receive = r.n_send.at[t - ATTN, k], r.n_recv.at[t - ATTN, k]
            return to_dp(part, part, send, receive, lax.rem(dp + k, ng))

        def near_join(t):
            total = part_of(t, z, core)[...].astype(F32)
            for k in range(1, nz):
                near_copy(t, k).wait_recv()
                total += shared[t][4][k].astype(F32)
            done_part(t, z, core)[...] = total.astype(BF16)
            for k in range(1, ng):
                all_copy(t, k, dp).start()

        def swap(t):
            for q in range(nx):
                swap_copy(t, q).start()

        def plane_one(t):
            for k in (3, 1, 2, 0):
                q = peer(k)
                swap_copy(t, q).wait_recv()
                add_to(half_of(t, q, core), swap_in(t, q))
                if k == 3:
                    for c in range(2):
                        plane_cross(t, c).start()

        def plane_two(t):
            for c in range(2):
                plane_cross(t, c).wait_recv()
                add_to(quarter(t, 2 - c, c), shared[t][3].at[2, c])
            for c in range(2):
                for k in (1, 2):
                    plane_copy(t, k, c).start()

        def line_start(t):
            for c in range(2):
                for k in (1, 2):
                    plane_copy(t, k, c).wait_recv()
                mine = quarter(t, 0, c)
                total = mine[...].astype(F32)
                for k in (1, 2):
                    total += shared[t][3][k - 1, c].astype(F32)
                mine[...] = total.astype(BF16)
            if t >= ATTN:
                for k in range(1, nz):
                    near_copy(t, k).start()
                return

            @pl.when(z == 0)
            def _():
                for d in reversed(range(1, nz)):
                    part_copy(t, d, 1).start()

            @pl.when(z == nz - 1)
            def _():
                for d in range(nz - 1):
                    part_copy(t, d, -1).start()

        def line_hop(t, h):
            @pl.when(z == h)
            def _():
                for d in reversed(range(h, nz)):
                    part_copy(t, d, 1).wait_recv()
                    add_to(part_of(t, d, core), shared[t][4].at[d + 1])
                    if d > h:
                        part_copy(t, d, 1).start()

            @pl.when(z == nz - 1 - h)
            def _():
                for d in range(nz - h):
                    part_copy(t, d, -1).wait_recv()
                    add_to(part_of(t, d, core), shared[t][4].at[d])
                    if d < nz - 1 - h:
                        part_copy(t, d, -1).start()

        def share_start(t):
            for d in range(nz):

                @pl.when(z == d)
                def _():
                    done_part(t, d, core)[...] = part_of(t, d, core)[...]
                    if d < nz - 1:
                        share_copy(t, d, 1).start()
                    if d > 0:
                        share_copy(t, d, -1).start()
                    give_copy(t, d, core).start()

        def share_hop(t, h):
            for d in range(nz):
                for step in (1, -1):
                    at = d + step * h
                    if 0 <= at < nz:

                        @pl.when(z == at)
                        def _():
                            share_copy(t, d, step).wait_recv()
                            if 0 <= at + step < nz:
                                share_copy(t, d, step).start()
                            give_copy(t, d, core).start()

        loads[0].wait()
        for c in range(2):
            span = pl.ds(c * half, half)
            normed, _ = norm_parts(r.tokv[span, :].astype(F32))
            r.u1[span, :] = (normed * r.g1[...] + r.b1[...]).astype(BF16)
        loads[1].wait()
        for i in range(3):
            part = mm(r.u1[...], r.wqkv[:, i * width : (i + 1) * width]).astype(BF16)
            r.qkv[i] = part * jnp.asarray(0.125, BF16) if i == 0 else part
        seg_row = jnp.broadcast_to(r.seg[...].astype(F32), (8, rows))
        seg_col = jnp.transpose(seg_row)[:, 0:1]
        r.du[...] = jnp.where(seg_col == seg_row[0:1, :], 0.0, -1e30)
        lane = lax.broadcasted_iota(jnp.int32, (1, PAIR), 1)
        masks = (
            jnp.where(lane < HD, 1.0, 0.0).astype(BF16),
            jnp.where(lane < HD, 0.0, 1.0).astype(BF16),
        )

        @pl.loop(0, width // PAIR)
        def _(pair):
            cols = tile(pair, PAIR)
            keys, values = r.qkv[1, :, cols], r.qkv[2, :, cols]
            for c in range(2):
                span = pl.ds(c * half, half)
                queries = r.qkv[0, span, cols]
                mixed = jnp.zeros((half, PAIR), F32)
                for h in range(2):
                    s = mm_nt(queries * masks[h], keys) + r.du[span, :]
                    e = jnp.exp(s - jnp.max(s, axis=1, keepdims=True))
                    p = (e * (1.0 / jnp.sum(e, axis=1, keepdims=True))).astype(BF16)
                    r.probs[pair * 2 + h, span, :] = p
                    mixed += mm(p, values * masks[h])
                r.ao[span, cols] = mixed.astype(BF16)

        for l in range(1, local):
            for k in range(1, nx):
                row_copy(1, l - 1, k, me).wait_send()
                row_copy(1, l, k, me).start()
        for i in (2, 3, 4):
            loads[i].wait()
        for c in range(2):
            span = pl.ds(c * half, half)
            x1 = r.tokv[span, :].astype(F32) + mm(r.ao[span, :], r.wo[...])
            r.x1[span, :] = x1
            normed, _ = norm_parts(x1)
            r.u2[span, :] = (normed * r.g2[...] + r.b2[...]).astype(BF16)
            r.x2[span, :] = x1

            @pl.loop(0, steps)
            def _(t):
                cols = tile(t, ft)
                act, slope = gelu_both(mm(r.u2[span, :], r.wup[:, cols]))
                act = act.astype(BF16)
                r.a2[span, cols] = act
                r.s2[span, cols] = slope.astype(BF16)
                r.x2[span, :] += mm(act, r.wdn[cols, :])

            normed, _ = norm_parts(r.x2[span, :])
            r.u3[span, :] = (normed * r.g3[...] + r.b3[...]).astype(BF16)

        def compact(l):
            for k in range(1, nx):
                r.out_u[peer(k), l] = mm(r.comp[peer(k), l], r.u3[...]).astype(BF16)
                if l == 0:
                    row_copy(0, l, k, me).start()
            r.in_u[me, l] = mm(r.comp[me, l], r.u3[...]).astype(BF16)

        for l in range(local):
            compact(l)
        for k in range(1, nx):
            rank_copy(k, peer(k)).wait_recv()
        r.small2[...] = jnp.zeros(r.small2.shape, F32)
        for l in range(local):
            routed = jnp.zeros((1, depth), F32)
            for j in range(nx):
                routed += jnp.where(r.sp_in[j, l : l + 1, :] >= 0.0, 1.0, 0.0)
            routed = jnp.sum(routed, axis=1, keepdims=True)
            kept = jnp.minimum(routed, float(capacity))
            spot = lax.broadcasted_iota(jnp.int32, (1, r.small2.shape[1]), 1)
            line = jnp.where(spot == 0, kept, jnp.where(spot == 1, routed - kept, 0.0))
            r.small2[8 + ep + l : 9 + ep + l, :] = line
        columns = [jnp.transpose(r.sp_in[j]) for j in range(nx)]
        for j in range(nx):
            r.rank[j] = jnp.full((8, depth), -1.0, F32)
            for l in range(local):
                mine = r.sp_in[j, l : l + 1, :]
                above = jnp.zeros((1, depth), F32)
                for column in columns:
                    above += jnp.sum(
                        jnp.where(column[:, l : l + 1] > mine, 1.0, 0.0), axis=0, keepdims=True
                    )
                keep = (mine >= 0.0) & (above < float(capacity))
                r.rank[j, l : l + 1, :] = jnp.where(keep, above, -1.0)

        row_id = lax.broadcasted_iota(jnp.int32, (room, depth), 0).astype(F32)

        def gather(source, target, l):
            total = jnp.zeros((room, width), F32)
            for j in range(nx):
                pick = jnp.where(row_id == r.rank[j, l : l + 1, :], 1.0, 0.0).astype(BF16)
                total += mm(pick, source[j, l])
            target[l] = total.astype(BF16)

        def fetch(l):
            for k in range(1, nx):
                row_copy(1, l, k, peer(k)).wait_recv()
            gather(r.in_z, r.dzr, l)
            for k in range(1, nx):
                row_copy(0, l, k, peer(k)).wait_recv()
            gather(r.in_u, r.xr, l)

        for k in range(1, nx):
            row_copy(1, local - 1, k, me).wait_send()
        for l in range(1, local):
            for k in range(1, nx):
                row_copy(0, l - 1, k, me).wait_send()
                row_copy(0, l, k, me).start()
        fetch(0)

        loads[5].wait()
        loads[6].wait()
        lane_e = lax.broadcasted_iota(jnp.int32, (room, ep), 1)
        router = r.wr[...].astype(F32)
        if ep > experts_all:
            spare = jnp.zeros((ep - experts_all, width), F32)
            router = jnp.concatenate([router, spare], axis=0)
        r.wrt[...] = router.astype(BF16)
        lane_id = lax.broadcasted_iota(jnp.int32, (depth, room), 1).astype(F32)

        def spread(j, l, found):
            ranks = jnp.transpose(r.rank[j])[:, l : l + 1]
            put = jnp.where(lane_id == ranks, 1.0, 0.0).astype(BF16)
            return mm(put, found[l]).astype(BF16)

        def send_rows(flow, l):
            found, source, target = ((r.xr, r.in_u, r.out_u), (r.dzr, r.in_z, r.out_z))[flow % 2]
            for k in range(1, nx):
                source[peer(k), l] = spread(peer(k), l, found)
                if flow == 3:
                    row_copy(flow, l, k, me).start()
            target[me, l] = spread(me, l, found)

        def gate_grads(j):
            r.gt_out[j] = jnp.zeros((8, depth), F32)
            for l in range(local):
                hit = row_id == r.rank[j, l : l + 1, :]
                line = jnp.sum(jnp.where(hit, r.dgate[l], 0.0), axis=0, keepdims=True)
                r.gt_out[j, l : l + 1, :] = line

        events = []
        for m in range(len(rightward)):
            events.append((FEED + STEP * max(0, m - WINDOW + 2), m, functools.partial(feed, m)))
            for h in range(1, nz):
                arrival = FEED + STEP * (m + 1) + LAG + HOP * (h - 1)
                events.append((arrival, m, functools.partial(hop, m, h)))
        events.sort(key=lambda event: event[0])

        def pump(now):
            while events and events[0][0] <= now and (events[0][1] < 0 or ready(events[0][1])):
                events.pop(0)[2]()

        clock = START
        for l in range(local):
            if l:
                fetch(l)
            rows_in = r.xr[l]
            r.xrt[...] = jnp.transpose(rows_in)
            logits = jnp.where(lane_e < experts_all, mm_nt(rows_in, r.wrt[...]), -1e30)
            e = jnp.exp(logits - jnp.max(logits, axis=1, keepdims=True))
            gate = jnp.sum(
                jnp.where(lane_e == me * local + l, e, 0.0), axis=1, keepdims=True
            ) / jnp.sum(e, axis=1, keepdims=True)
            r.dyr[...] = (r.dzr[l].astype(F32) * gate).astype(BF16)
            for i, d in enumerate(far_first):
                cols = pl.ds(d * ft, ft)
                for c in range(2):
                    side = pl.ds(c * (ft // 2), ft // 2)
                    part = pl.ds(d * ft + c * (ft // 2), ft // 2)
                    act, slope = gelu_both(mm(r.xr[l], r.eup[l, :, part]))
                    r.act[:, side] = act.astype(BF16)
                    r.dh[:, side] = (mm_nt(r.dyr[...], r.edn[l, part, :]) * slope).astype(BF16)
                y = mm(r.act[...], r.edn[l, cols, :])
                dx = mm_nt(r.dh[...], r.eup[l, :, cols])
                if i:
                    r.acc_a[...] += y
                    r.acc_b[...] += dx
                else:
                    r.acc_a[...] = y
                    r.acc_b[...] = dx
                r.edn[l, cols, :] = mm_tn(r.act[...], r.dyr[...]).astype(BF16)
                r.eup[l, :, cols] = mm(r.xrt[...], r.dh[...]).astype(BF16)
                mate_copy(DOWN, l, d).start()
                for _ in range(1 + l):
                    if waiting:
                        join(*waiting.pop(0))
                waiting.append((DOWN, l, d))
                clock += TILE
                pump(clock)
            for d in far_first:
                mate_copy(UP, l, d).start()
                waiting.append((UP, l, d))
            y = r.acc_a[...].astype(BF16).astype(F32)
            r.dgate[l] = jnp.sum(r.dzr[l].astype(F32) * y, axis=1, keepdims=True)
            r.xr[l] = (y * gate).astype(BF16)
            r.dzr[l] = r.acc_b[...].astype(BF16)
            if l == 0:
                for k in range(1, nx):
                    row_copy(0, local - 1, k, me).wait_send()
            send_rows(3, l)
            pump(clock + 1.0)

        while waiting:
            join(*waiting.pop(0))
        pl.semaphore_signal(r.credit, inc=1, device_id={DP: mate}, device_id_type=MESH)
        for k in range(1, nx):
            gate_grads(peer(k))
            gt_copy(k, me).start()
        gate_grads(me)
        r.gt_in[me] = r.gt_out[me]
        pump(AFTER_EXPERTS)
        for l in range(local):
            send_rows(2, l)
        pump(BEFORE_BACK)

        for k in range(1, nx):
            gt_copy(k, peer(k)).wait_recv()
        r.gt_sum[...] = jnp.zeros((ep, rows), F32)
        for j in range(nx):
            column = jnp.transpose(r.gt_in[j])
            for l in range(local):
                spots = r.comp[j, l].astype(F32) * column[:, l : l + 1]
                line = jnp.sum(spots, axis=0, keepdims=True)
                r.gt_sum[j * local + l : j * local + l + 1, :] = line
        dgates = r.gt_sum[...]
        for l in range(local):
            for k in range(1, nx):
                row_copy(3, l, k, peer(k)).wait_recv()
        def at_home(source, c):
            chosen = jnp.concatenate(
                [r.comp[j, l, :, pl.ds(c * half, half)] for j in range(nx) for l in range(local)],
                axis=0,
            )
            found = jnp.concatenate(
                [source[j, l] for j in range(nx) for l in range(local)], axis=0
            )
            return mm_tn(chosen, found)

        row_e = lax.broadcasted_iota(jnp.int32, (ep, rows), 0)
        u3 = r.u3[...]
        logits = jnp.where(row_e < experts_all, mm_nt(r.wrt[...], u3), -1e30)
        e = jnp.exp(logits - jnp.max(logits, axis=0, keepdims=True))
        gates = e / jnp.sum(e, axis=0, keepdims=True)
        dlogits = (
            gates * (dgates - jnp.sum(gates * dgates, axis=0, keepdims=True))
        ).astype(BF16)
        r.small1[8 : 8 + ep, :] = mm(dlogits, u3)
        for c in range(2):
            span = pl.ds(c * half, half)
            r.du[span, :] = at_home(r.out_z, c) + mm_tn(
                dlogits[:, c * half : (c + 1) * half], r.wrt[...]
            )

        def norm_step(value, gain, base, line, pieces=2):
            size = rows // pieces

            def one(i, sums):
                span = tile(i, size)
                dv, dgain, dbias = norm_back(
                    value[span, :].astype(F32), r.du[span, :], gain[...]
                )
                r.dx[span, :] = base(span) + dv
                return sums[0] + dgain, sums[1] + dbias

            zero = jnp.zeros((1, width), F32)
            dgain, dbias = lax.fori_loop(0, pieces, one, (zero, zero))
            r.small1[line : line + 1, :] = dgain
            r.small1[line + 1 : line + 2, :] = dbias

        r.small1[0:8, :] = jnp.zeros((8, width), F32)
        norm_step(r.x2, r.g3, lambda span: r.dz[span, :].astype(F32), 4)
        r.low[...] = r.dx[...].astype(BF16)
        r.trans[...] = jnp.transpose(r.u2[...])
        r.du[...] = jnp.zeros((rows, width), F32)

        pump(AFTER_NORM)

        @pl.loop(0, steps)
        def _(t):
            cols = tile(t, ft)
            dm = r.low[...]
            dh = (mm_nt(dm, r.wdn[cols, :]) * r.s2[:, cols].astype(F32)).astype(BF16)
            r.s2[:, cols] = dh
            r.du[...] += mm_nt(dh, r.wup[:, cols])

        pump(AFTER_MLP)

        @pl.loop(0, steps)
        def _(t):
            cols = tile(t, ft)
            r.wdn[cols, :] = mm_tn(r.a2[:, cols], r.low[...]).astype(BF16)
            r.wup[:, cols] = mm(r.trans[...], r.s2[:, cols]).astype(BF16)

        pl.semaphore_wait(r.credit, 1)
        swap(DOWN)
        swap(UP)
        pump(AFTER_MLP_GRADS)
        norm_step(r.x1, r.g2, lambda span: r.dx[span, :], 2)
        do = r.dx[...].astype(BF16)
        r.low[...] = mm_nt(do, r.wo[...]).astype(BF16)
        r.wo[...] = mm_tn(r.ao[...], do).astype(BF16)
        swap(ATTN)
        plane_one(DOWN)
        plane_one(UP)
        pump(AFTER_OUT)

        for pair in range(width // PAIR):
            cols = pl.ds(pair * PAIR, PAIR)
            keys, values = r.qkv[1, :, cols], r.qkv[2, :, cols]
            dk = jnp.zeros((rows, PAIR), F32)
            dv = jnp.zeros((rows, PAIR), F32)
            for c in range(2):
                span = pl.ds(c * half, half)
                queries = r.qkv[0, span, cols]
                dao = r.low[span, cols]
                dq = jnp.zeros((half, PAIR), F32)
                for h in range(2):
                    p = r.probs[pair * 2 + h, span, :]
                    mine = dao * masks[h]
                    weighed = p.astype(F32) * mm_nt(mine, values)
                    total = jnp.sum(weighed, axis=1, keepdims=True)
                    ds = (weighed - p.astype(F32) * total).astype(BF16)
                    dq += mm(ds, keys * masks[h])
                    dk += mm_tn(ds, queries * masks[h])
                    dv += mm_tn(p, mine)
                r.qkv[0, span, cols] = (dq * 0.125).astype(BF16)
            r.qkv[1, :, cols] = dk.astype(BF16)
            r.qkv[2, :, cols] = dv.astype(BF16)
            if pair == 0:
                plane_two(DOWN)
            if pair == 1:
                plane_two(UP)
                plane_one(ATTN)
            if pair == 2:
                plane_two(ATTN)
            pump(AFTER_OUT + PAIR_TIME * (pair + 1))

        r.trans[...] = jnp.transpose(r.u1[...])
        du = jnp.zeros((rows, width), F32)
        for i in range(3):
            cols = slice(i * width, (i + 1) * width)
            du += mm_nt(r.qkv[i], r.wqkv[:, cols])
            r.wqkv[:, cols] = mm(r.trans[...], r.qkv[i]).astype(BF16)
        swap(QKV)
        r.du[...] = du
        norm_step(r.tokv, r.g1, lambda span: r.dx[span, :], 0)
        early = [pltpu.make_async_copy(r.dx, r.gtok, r.load_sem.at[8])]
        early[0].start()
        plane_one(QKV)
        line_start(DOWN)
        line_start(UP)
        line_start(ATTN)

        wide = width // nx

        def small_copy(k, slot):
            start = pl.multiple_of(peer(k) * wide, wide)
            return direct(r.small1.at[:, pl.ds(start, wide)], r.s1_in.at[slot], 2, k)

        for k in range(1, nx):
            small_copy(k, me).start()

        def start_y():
            for l in range(local):
                for k in range(1, nx):
                    row_copy(2, l, k, me).start()

        def finish_y():
            for l in range(local):
                for k in range(1, nx):
                    row_copy(2, l, k, peer(k)).wait_recv()
            for c in range(2):
                span = pl.ds(c * half, half)
                r.u3[span, :] = (r.x2[span, :] + at_home(r.out_u, c)).astype(BF16)
            early.append(pltpu.make_async_copy(r.u3, r.out, r.load_sem.at[9]))
            early[1].start()


        for k in range(1, nx):
            small_copy(k, peer(k)).wait_recv()
        total = r.small1[:, pl.ds(pl.multiple_of(me * wide, wide), wide)]
        for k in range(1, nx):
            total += r.s1_in[peer(k)]
        r.small2[0 : 8 + ep, :] = total

        def small2_copy(k, slot):
            return to_dp(
                r.small2,
                r.s2_in.at[slot],
                r.s_send.at[k],
                r.s_recv.at[k],
                lax.rem(dp + k, ng),
            )

        for k in range(1, ng):
            small2_copy(k, dp).start()
        r.s2_in[dp] = r.small2[...]

        def later(offset, step, *args):
            events.append((LINE + offset, -1, functools.partial(step, *args)))

        later(3.0, plane_two, QKV)
        later(8.0, line_start, QKV)
        later(9.0, near_join, ATTN)
        later(14.0, near_join, QKV)
        later(8.5, start_y)
        later(26.0, finish_y)
        for t in (DOWN, UP):
            for h in range(1, nz):
                later(LINE_HOP * h, line_hop, t, h)
                later(LINE_HOP * (nz - 1) + SHARE_HOP * h, share_hop, t, h)
            later(LINE_HOP * (nz - 1) + 0.5, share_start, t)
        events.sort(key=lambda event: event[0])
        pump(math.inf)

        for k in range(1, ng):
            small2_copy(k, lax.rem(dp + ng - k, ng)).wait_recv()
        total = r.s2_in[0]
        for j in range(1, ng):
            total += r.s2_in[j]
        r.small[...] = total

        saves = []
        for kind, target in ((DOWN, r.gedn), (UP, r.geup)):
            for l in range(local):
                saves.append((block(kind, l, z, core), target.at[l]))
        for t, target in enumerate((r.gdn, r.gup, r.go, r.gqkv)):
            if t >= ATTN:
                for k in range(1, ng):
                    all_copy(t, k, lax.rem(dp + ng - k, ng)).wait_recv()
            else:
                for d in range(nz):
                    give_copy(t, d, 1 - core).wait_recv()
            saves.append((done[t], target))
        saves = [
            pltpu.make_async_copy(src, dst, r.load_sem.at[i])
            for i, (src, dst) in enumerate(saves)
        ]
        for copy in saves:
            copy.start()
        for copy in saves + early:
            copy.wait()

        for k in range(1, nx):
            rank_copy(k, me).wait_send()
            gt_copy(k, me).wait_send()
            small_copy(k, me).wait_send()
            for l in range(local):
                row_copy(2, l, k, me).wait_send()
                row_copy(3, l, k, me).wait_send()
        for k in range(1, ng):
            small2_copy(k, dp).wait_send()
        for l in range(local):
            for kind in (DOWN, UP):
                for d in range(nz):
                    mate_copy(kind, l, d).wait_send()
        for m, (right, left) in enumerate(zip(rightward, leftward)):
            last = m >= len(rightward) - WINDOW

            @pl.when((z < right[2]) & (last | (z > 0)))
            def _():
                right_copy(*right).wait_send()

            @pl.when((z > left[2]) & (last | (z < nz - 1)))
            def _():
                left_copy(*left).wait_send()

        for t in range(4):
            for q in range(nx):
                swap_copy(t, q).wait_send()
            for c in range(2):
                plane_cross(t, c).wait_send()
                for k in (1, 2):
                    plane_copy(t, k, c).wait_send()
            if t >= ATTN:
                for k in range(1, nz):
                    near_copy(t, k).wait_send()
                for k in range(1, ng):
                    all_copy(t, k, dp).wait_send()
                continue
            for d in range(nz):
                give_copy(t, d, core).wait_send()

                @pl.when(z != d)
                def _():
                    part_copy(t, d, 1).wait_send()

                @pl.when((z >= d) & (z < nz - 1))
                def _():
                    share_copy(t, d, 1).wait_send()

                @pl.when((z <= d) & (z > 0))
                def _():
                    share_copy(t, d, -1).wait_send()

    return kernel


def fits(scratch):
    total = 0
    for buffer in scratch.values():
        if buffer.dtype in (F32, BF16):
            lead, (high, wide) = buffer.shape[:-2], buffer.shape[-2:]
            lanes = (wide + 127) // 128 * 128
            total += math.prod(lead) * high * lanes * jnp.dtype(buffer.dtype).itemsize
    return total < VMEM_PLAN


def shards(*args):
    got = kernel_shards(*args)
    return plain_shards(*args) if got is None else got


def kernel_shards(
    tokens,
    segments,
    experts,
    priority,
    cotangent,
    ln1_gain,
    ln1_bias,
    w_qkv,
    w_attn_out,
    ln2_gain,
    ln2_bias,
    w_up,
    w_down,
    ln3_gain,
    ln3_bias,
    w_router,
    expert_up,
    expert_down,
):
    rows, width = tokens.shape
    local, _, ff = expert_up.shape
    experts_all = w_router.shape[1]
    nx, ng = lax.axis_size(EXPERT), lax.axis_size(DP)
    nz = ng // 2
    capacity = (21 * rows + 10 * local - 1) // (10 * local)
    room = (capacity + 15) // 16 * 16
    heads = width // HD
    depth = 3 * rows // experts_all
    ep = max(16, experts_all)
    fb, wb = ff // ng, width // ng
    line = lambda v: v.reshape(1, width)
    hbm = pl.BlockSpec(memory_space=pl.ANY)
    vmem = pl.BlockSpec(memory_space=pltpu.VMEM)
    dma = pltpu.SemaphoreType.DMA
    units = local * 2 * nz

    def by_plane(high, wide):
        return pltpu.VMEM((3, 2, high // nx // 4, wide), BF16)

    def by_line(high, wide):
        return pltpu.VMEM((nz + 1, high // nx // 2 // nz, wide), BF16)

    scratch = dict(
        tokv=pltpu.VMEM((rows, width), BF16),
        wqkv=pltpu.VMEM(w_qkv.shape, BF16),
        wo=pltpu.VMEM(w_attn_out.shape, BF16),
        wup=pltpu.VMEM(w_up.shape, BF16),
        wdn=pltpu.VMEM(w_down.shape, BF16),
        eup=pltpu.VMEM(expert_up.shape, BF16),
        edn=pltpu.VMEM(expert_down.shape, BF16),
        wrt=pltpu.VMEM((ep, width), BF16),
        u1=pltpu.VMEM((rows, width), BF16),
        qkv=pltpu.VMEM((3, rows, width), BF16),
        probs=pltpu.VMEM((heads, rows, rows), BF16),
        ao=pltpu.VMEM((rows, width), BF16),
        x1=pltpu.VMEM((rows, width), F32),
        u2=pltpu.VMEM((rows, width), BF16),
        a2=pltpu.VMEM((rows, ff), BF16),
        s2=pltpu.VMEM((rows, ff), BF16),
        x2=pltpu.VMEM((rows, width), F32),
        u3=pltpu.VMEM((rows, width), BF16),
        dz=pltpu.VMEM((rows, width), BF16),
        comp=pltpu.VMEM((nx, local, depth, rows), BF16),
        out_u=pltpu.VMEM((nx, local, depth, width), BF16),
        in_u=pltpu.VMEM((nx, local, depth, width), BF16),
        out_z=pltpu.VMEM((nx, local, depth, width), BF16),
        in_z=pltpu.VMEM((nx, local, depth, width), BF16),
        sp_out=pltpu.VMEM((nx, 8, depth), F32),
        sp_in=pltpu.VMEM((nx, 8, depth), F32),
        rank=pltpu.VMEM((nx, 8, depth), F32),
        act=pltpu.VMEM((room, ff // nz), BF16),
        dh=pltpu.VMEM((room, ff // nz), BF16),
        acc_a=pltpu.VMEM((room, width), F32),
        acc_b=pltpu.VMEM((room, width), F32),
        xr=pltpu.VMEM((local, room, width), BF16),
        xrt=pltpu.VMEM((width, room), BF16),
        dzr=pltpu.VMEM((local, room, width), BF16),
        dyr=pltpu.VMEM((room, width), BF16),
        dgate=pltpu.VMEM((local, room, 1), F32),
        gt_out=pltpu.VMEM((nx, 8, depth), F32),
        gt_in=pltpu.VMEM((nx, 8, depth), F32),
        gt_sum=pltpu.VMEM((ep, rows), F32),
        small1=pltpu.VMEM((8 + ep, width), F32),
        small2=pltpu.VMEM((16 + ep, width // nx), F32),
        s1_in=pltpu.VMEM((nx, 8 + ep, width // nx), F32),
        s2_in=pltpu.VMEM((ng, 16 + ep, width // nx), F32),
        xdn=pltpu.VMEM((local, ff // 2, width), BF16),
        xup=pltpu.VMEM((local, width // 2, ff), BF16),
        zdn=pltpu.VMEM((local, nz + 1, fb, width), BF16),
        zup=pltpu.VMEM((local, nz + 1, wb, ff), BF16),
        bdn=by_plane(ff, width),
        bup=by_plane(width, ff),
        bo=by_plane(width, width),
        bqkv=by_plane(width, 3 * width),
        cdn=by_line(ff, width),
        cup=by_line(width, ff),
        co=by_line(width, width),
        cqkv=by_line(width, 3 * width),
        credit=pltpu.SemaphoreType.REGULAR,
        load_sem=dma((16,)),
        send_sem=dma((3, nx)),
        recv_sem=dma((3, nx)),
        row_send=dma((4 * local * nx,)),
        row_recv=dma((4 * local * nx,)),
        x_send=dma((units,)),
        x_recv=dma((units,)),
        z_send=dma((units,)),
        z_recv=dma((units, 2)),
        a_send=dma((4, nx)),
        a_recv=dma((4, nx)),
        b_send=dma((4, 6)),
        b_recv=dma((4, 6)),
        c_send=dma((4, nz)),
        c_recv=dma((4, nz, 2)),
        g_send=dma((4, nz, 2)),
        g_recv=dma((4, nz)),
        p_send=dma((4, nz)),
        p_recv=dma((4, nz)),
        n_send=dma((2, ng)),
        n_recv=dma((2, ng)),
        s_send=dma((ng,)),
        s_recv=dma((ng,)),
    )
    if nx != 4 or not fits(scratch):
        return None
    sds = jax.ShapeDtypeStruct
    outs = dict(
        out=sds((rows, width), BF16),
        gtok=sds((rows, width), F32),
        small=sds((16 + ep, width // nx), F32),
        gdn=sds((ff // nx, width), BF16),
        gup=sds((width // nx, ff), BF16),
        go=sds((width // nx, width), BF16),
        gqkv=sds((width // nx, 3 * width), BF16),
        geup=sds((local, wb, ff), BF16),
        gedn=sds((local, fb, width), BF16),
    )
    got = pl.pallas_call(
        make_kernel(
            rows, width, ff, local, experts_all, nx, ng, capacity, room, depth, list(scratch)
        ),
        out_shape=tuple(outs[name] for name in NAMES_OUT),
        in_specs=[hbm, hbm] + [vmem] * 10 + [hbm] * 6,
        out_specs=(hbm, hbm, vmem) + (hbm,) * 6,
        scratch_shapes=list(scratch.values()),
        compiler_params=pltpu.CompilerParams(
            collective_id=0, has_side_effects=True, vmem_limit_bytes=63 << 20
        ),
    )(
        tokens,
        cotangent,
        experts.T,
        priority.T,
        segments.reshape(1, rows),
        line(ln1_gain),
        line(ln1_bias),
        line(ln2_gain),
        line(ln2_bias),
        line(ln3_gain),
        line(ln3_bias),
        w_router.T,
        w_qkv,
        w_attn_out,
        w_up,
        w_down,
        expert_up,
        expert_down,
    )
    return finish(got, experts_all, local)


def finish(got, experts_all, local):
    out, gtok, small, *low = got
    wide = small.shape[1]
    ep = max(16, experts_all)

    def kernel(*refs):
        count = len(low)
        out_in, gtok_in, small_in = refs[:3]
        low_in, refs = refs[3 : 3 + count], refs[3 + count :]
        out_to, gtok_to = refs[:2]
        lines, router, counts = refs[2:8], refs[8], refs[9]
        high_out, refs = refs[10 : 10 + count], refs[10 + count :]
        short, long, sem = refs[:count], refs[count : 2 * count], refs[2 * count]
        held = refs[2 * count + 1 :]
        through = [
            pltpu.make_async_copy(out_in, held[0], sem.at[0]),
            pltpu.make_async_copy(gtok_in, held[1], sem.at[1]),
        ]
        loads = [
            pltpu.make_async_copy(low_in[i], short[i], sem.at[2 + i]) for i in range(count)
        ]
        for copy in loads + through:
            copy.start()
        copies = []
        for i in range(6):
            lines[i][...] = small_in[i : i + 1, :]
        router[...] = jnp.transpose(small_in[8 : 8 + experts_all, :])
        counts[...] = small_in[8 + ep : 8 + ep + local, 0:2]
        for i in range(count):
            loads[i].wait()
            long[i][...] = short[i][...].astype(F32)
            copies.append(pltpu.make_async_copy(long[i], high_out[i], sem.at[2 + count + i]))
            copies[-1].start()
        for i, target in enumerate((out_to, gtok_to)):
            through[i].wait()
            copies.append(pltpu.make_async_copy(held[i], target, sem.at[i]))
            copies[-1].start()
        for copy in copies:
            copy.wait()

    sds = jax.ShapeDtypeStruct
    hbm = pl.BlockSpec(memory_space=pl.ANY)
    vmem = pl.BlockSpec(memory_space=pltpu.VMEM)
    full = pl.pallas_call(
        kernel,
        out_shape=(
            sds(out.shape, BF16),
            sds(gtok.shape, F32),
            *[sds((1, wide), F32)] * 6,
            sds((wide, experts_all), F32),
            sds((local, 2), F32),
            *[sds(v.shape, F32) for v in low],
        ),
        in_specs=[hbm, hbm, vmem] + [hbm] * len(low),
        out_specs=(hbm, hbm) + (vmem,) * 8 + (hbm,) * len(low),
        scratch_shapes=[
            *[pltpu.VMEM(v.shape, BF16) for v in low],
            *[pltpu.VMEM(v.shape, F32) for v in low],
            pltpu.SemaphoreType.DMA((2 + 2 * len(low),)),
            pltpu.VMEM(out.shape, BF16),
            pltpu.VMEM(gtok.shape, F32),
        ],
        compiler_params=pltpu.CompilerParams(vmem_limit_bytes=56 << 20),
    )(*got)
    norms = [v.reshape(wide) for v in full[2:8]]
    router, counts = full[8:10]
    gdn, gup, go, gqkv, geup, gedn = full[10:]
    return (
        *full[:2],
        *norms[:2],
        gqkv,
        go,
        *norms[2:4],
        gup,
        gdn,
        *norms[4:],
        router,
        geup,
        gedn,
        counts,
    )


def solution(mesh):
    both = (DP, EXPERT)
    token = P(both, None)
    in_specs = (token, P(both), token, token, token) + (P(),) * 11
    in_specs += (P(EXPERT, None, None),) * 2
    out_specs = (
        token,
        token,
        P(EXPERT),
        P(EXPERT),
        P(EXPERT, None),
        P(EXPERT, None),
        P(EXPERT),
        P(EXPERT),
        P(EXPERT, None),
        P(EXPERT, None),
        P(EXPERT),
        P(EXPERT),
        P(EXPERT, None),
        P(EXPERT, DP, None),
        P(EXPERT, DP, None),
        P(EXPERT, None),
    )
    return jax.shard_map(shards, mesh=mesh, in_specs=in_specs, out_specs=out_specs, check_vma=False)
```

```python
import functools
import math

import jax
import jax.numpy as jnp
from jax import lax
from jax.experimental import pallas as pl
from jax.experimental.pallas import tpu as pltpu
from jax.sharding import PartitionSpec as P

MESH = pl.DeviceIdType.MESH
F32 = jnp.float32
BF16 = jnp.bfloat16
HD = 64
DP = "dp"
EXPERT = "expert"
VMEM_PLAN = 57 << 20
PAIR = 2 * HD
epsilon = 1e-06
GELU_C = 0.7978845608028654
GELU_A = 0.044715


HEADS = 8
TOP = 2
SEQ = 512
score_scale = 0.125
masked_score = -1e30


def norm_forward(values, norm_gain, norm_shift):
    centre = values - jnp.mean(values, axis=1, keepdims=True)
    inverse = lax.rsqrt(jnp.mean(centre * centre, axis=1, keepdims=True) + epsilon)
    normed = centre * inverse
    return (normed * norm_gain + norm_shift, normed, inverse)


def norm_backward(upstream, normed, inverse, norm_gain):
    scaled = upstream * norm_gain
    inner = (
        scaled
        - jnp.mean(scaled, axis=1, keepdims=True)
        - normed * jnp.mean(scaled * normed, axis=1, keepdims=True)
    )
    return (inverse * inner, jnp.sum(upstream * normed, axis=0), jnp.sum(upstream, axis=0))


def gelu_tanh(values):
    return jax.nn.gelu(values, approximate=True)


def gelu_pull(values, upstream):
    return jax.vjp(gelu_tanh, values)[1](upstream)[0]


def masked_scores(query_rows, key_rows, query_seg, key_seg):
    raw_scores = (
        jnp.einsum("qhd,khd->hqk", query_rows, key_rows, preferred_element_type=jnp.float32)
        * score_scale
    )
    same_image = query_seg[:, None] == key_seg[None, :]
    return jnp.where(same_image[None], raw_scores, masked_score)


def attend_forward(queries, key_rows, value_rows, seg_ids):
    outputs, log_sums = ([], [])
    scores = masked_scores(queries, key_rows, seg_ids, seg_ids)
    row_peak = jnp.max(scores, axis=2, keepdims=True)
    exp_scores = jnp.exp(scores - row_peak)
    row_total = jnp.sum(exp_scores, axis=2, keepdims=True)
    attn_probs = (exp_scores / row_total).astype(jnp.bfloat16)
    outputs.append(
        jnp.einsum("hqk,khd->qhd", attn_probs, value_rows, preferred_element_type=jnp.float32)
    )
    log_sums.append(row_peak + jnp.log(row_total))
    return (outputs[0], log_sums[0])


def attend_backward(queries, key_rows, value_rows, seg_ids, log_sums, upstream):
    scores = masked_scores(queries, key_rows, seg_ids, seg_ids)
    attn_probs = jnp.exp(scores - log_sums)
    grad_values = jnp.einsum(
        "hqk,qhd->khd",
        attn_probs.astype(jnp.bfloat16),
        upstream,
        preferred_element_type=jnp.float32,
    )
    grad_probs = jnp.einsum(
        "qhd,khd->hqk", upstream, value_rows, preferred_element_type=jnp.float32
    )
    centred = grad_probs - jnp.sum(attn_probs * grad_probs, axis=2, keepdims=True)
    grad_scores = (attn_probs * centred).astype(jnp.bfloat16)
    grad_queries = (
        jnp.einsum("hqk,khd->qhd", grad_scores, key_rows, preferred_element_type=jnp.float32)
        * score_scale
    )
    grad_keys = (
        jnp.einsum("hqk,qhd->khd", grad_scores, queries, preferred_element_type=jnp.float32)
        * score_scale
    )
    return (grad_queries, grad_keys, grad_values)


def pick_rows(table, index_rows):
    return table[index_rows]


def plain_shards(
    tokens,
    segments,
    experts,
    priority,
    cotangent,
    ln1_gain,
    ln1_bias,
    w_qkv,
    w_attn_out,
    ln2_gain,
    ln2_bias,
    w_up,
    w_down,
    ln3_gain,
    ln3_bias,
    w_router,
    expert_up,
    expert_down,
):
    row_count, width = tokens.shape
    seq_count = row_count // SEQ
    expert_total = w_router.shape[1]
    local_experts = expert_up.shape[0]
    owner_count = lax.axis_size(EXPERT)
    slot_depth = 3 * row_count // expert_total
    capacity = (21 * row_count + 10 * local_experts - 1) // (10 * local_experts)
    arrive_rows = owner_count * slot_depth
    buffer_rows = local_experts * arrive_rows
    pick_count = row_count * TOP
    rank_span = pick_count * owner_count
    labels = jnp.arange(expert_total, dtype=jnp.int32)
    x_in = tokens.astype(jnp.float32)
    u1, normed1, inverse1 = norm_forward(x_in, ln1_gain, ln1_bias)
    u1_low = u1.astype(jnp.bfloat16)
    qkv_low = jnp.dot(u1_low, w_qkv, preferred_element_type=jnp.float32).astype(jnp.bfloat16)
    qkv_seq = qkv_low.reshape(seq_count, SEQ, 3, HEADS, HD)
    seg_seq = segments.reshape(seq_count, SEQ)
    mixed_parts, lse_parts = ([], [])
    seq_index = 0
    mixed_one, lse_one = attend_forward(
        qkv_seq[seq_index, :, 0],
        qkv_seq[seq_index, :, 1],
        qkv_seq[seq_index, :, 2],
        seg_seq[seq_index],
    )
    mixed_parts.append(mixed_one)
    lse_parts.append(lse_one)
    mixed_low = mixed_parts[0].reshape(row_count, width).astype(jnp.bfloat16)
    x1 = x_in + jnp.dot(mixed_low, w_attn_out, preferred_element_type=jnp.float32)
    u2, normed2, inverse2 = norm_forward(x1, ln2_gain, ln2_bias)
    u2_low = u2.astype(jnp.bfloat16)
    hidden2 = jnp.dot(u2_low, w_up, preferred_element_type=jnp.float32)
    active2 = gelu_tanh(hidden2).astype(jnp.bfloat16)
    x2 = x1 + jnp.dot(active2, w_down, preferred_element_type=jnp.float32)
    u3, normed3, inverse3 = norm_forward(x2, ln3_gain, ln3_bias)
    u3_low = u3.astype(jnp.bfloat16)
    logits = jnp.dot(u3_low, w_router, preferred_element_type=jnp.float32)
    exp_logits = jnp.exp(logits - jnp.max(logits, axis=1, keepdims=True))
    gates = exp_logits / jnp.sum(exp_logits, axis=1, keepdims=True)
    flat_ids = experts.reshape(-1)
    flat_ranks = priority.reshape(-1)
    hits = flat_ids[:, None] == labels[None, :]
    all_ids, all_ranks = (
        lax.all_gather(experts, EXPERT, axis=0, tiled=True),
        lax.all_gather(priority, EXPERT, axis=0, tiled=True),
    )
    id_at_rank = (
        jnp.zeros((rank_span,), jnp.int32).at[all_ranks.reshape(-1)].set(all_ids.reshape(-1))
    )
    marks = (id_at_rank[:, None] == labels[None, :]).astype(jnp.int32)
    above = jnp.cumsum(marks[::-1], axis=0)[::-1]
    kept_mask = above[flat_ranks, flat_ids] <= capacity
    chosen = hits & kept_mask[:, None]
    running = jnp.cumsum(chosen.astype(jnp.int32), axis=0) - 1
    slot_of = jnp.sum(jnp.where(chosen, running, 0), axis=1)
    target = (
        flat_ids % local_experts * arrive_rows + flat_ids // local_experts * slot_depth + slot_of
    )
    target = jnp.where(kept_mask, target, buffer_rows)
    source_pick = (
        jnp.full((buffer_rows,), pick_count, jnp.int32)
        .at[target]
        .set(jnp.arange(pick_count, dtype=jnp.int32), mode="drop")
    )
    send_flags = (
        (source_pick < pick_count)
        .astype(jnp.bfloat16)
        .reshape(local_experts, owner_count, slot_depth)
    )
    u3_pad = jnp.concatenate([u3_low, jnp.zeros((1, width), jnp.bfloat16)], axis=0)
    send_rows = u3_pad[source_pick // TOP].reshape(local_experts, owner_count, slot_depth, width)
    kept_total = jnp.sum(chosen, axis=0).astype(jnp.float32)
    routed = jnp.sum(hits, axis=0).astype(jnp.float32)
    counts = jnp.stack([kept_total, routed - kept_total], axis=1)
    recv_rows, recv_flags = (
        lax.all_to_all(send_rows, EXPERT, split_axis=1, concat_axis=1, tiled=True),
        lax.all_to_all(send_flags, EXPERT, split_axis=1, concat_axis=1, tiled=True),
    )
    recv_rows = recv_rows.reshape(local_experts, arrive_rows, width)
    valid = recv_flags.reshape(local_experts, arrive_rows) > 0
    places = jnp.cumsum(valid.astype(jnp.int32), axis=1) - 1
    places = jnp.where(valid, places, capacity)
    filler = jnp.arange(arrive_rows, dtype=jnp.int32)
    gather_index = jax.vmap(
        lambda spots: jnp.full((capacity,), arrive_rows, jnp.int32)
        .at[spots]
        .set(filler, mode="drop")
    )(places)
    zero_row = jnp.zeros((local_experts, 1, width), jnp.bfloat16)
    expert_in = jax.vmap(pick_rows)(jnp.concatenate([recv_rows, zero_row], axis=1), gather_index)
    expert_hidden = jnp.einsum(
        "ecd,edf->ecf", expert_in, expert_up, preferred_element_type=jnp.float32
    )
    expert_act = gelu_tanh(expert_hidden).astype(jnp.bfloat16)
    expert_out = jnp.einsum(
        "ecf,efd->ecd", expert_act, expert_down, preferred_element_type=jnp.float32
    ).astype(jnp.bfloat16)
    back_rows = jax.vmap(pick_rows)(jnp.concatenate([expert_out, zero_row], axis=1), places)
    returned = lax.all_to_all(
        back_rows.reshape(local_experts, owner_count, slot_depth, width),
        EXPERT,
        split_axis=1,
        concat_axis=1,
        tiled=True,
    )
    returned_pad = jnp.concatenate(
        [returned.reshape(buffer_rows, width), jnp.zeros((1, width), jnp.bfloat16)], axis=0
    )
    y_pair = returned_pad[target].reshape(row_count, TOP, width).astype(jnp.float32)
    pair_hit = experts[:, :, None] == labels[None, None, :]
    gate_pick = jnp.sum(jnp.where(pair_hit, gates[:, None, :], 0.0), axis=2)
    x3 = x2 + jnp.sum(gate_pick[:, :, None] * y_pair, axis=1)
    output = x3.astype(jnp.bfloat16)
    grad_out = cotangent.astype(jnp.float32)
    grad_y = (
        (gate_pick[:, :, None] * grad_out[:, None, :])
        .reshape(pick_count, width)
        .astype(jnp.bfloat16)
    )
    grad_y_pad = jnp.concatenate([grad_y, jnp.zeros((1, width), jnp.bfloat16)], axis=0)
    grad_send = grad_y_pad[source_pick].reshape(local_experts, owner_count, slot_depth, width)
    grad_recv = lax.all_to_all(
        grad_send, EXPERT, split_axis=1, concat_axis=1, tiled=True
    ).reshape(local_experts, arrive_rows, width)
    grad_expert_y = jax.vmap(pick_rows)(
        jnp.concatenate([grad_recv, zero_row], axis=1), gather_index
    )
    grad_expert_down = jnp.einsum(
        "ecf,ecd->efd", expert_act, grad_expert_y, preferred_element_type=jnp.float32
    )
    grad_expert_act = jnp.einsum(
        "ecd,efd->ecf", grad_expert_y, expert_down, preferred_element_type=jnp.float32
    )
    grad_expert_hidden = gelu_pull(expert_hidden, grad_expert_act).astype(jnp.bfloat16)
    grad_expert_up = jnp.einsum(
        "ecd,ecf->edf", expert_in, grad_expert_hidden, preferred_element_type=jnp.float32
    )
    grad_expert_in = jnp.einsum(
        "ecf,edf->ecd", grad_expert_hidden, expert_up, preferred_element_type=jnp.float32
    ).astype(jnp.bfloat16)
    grad_back = jax.vmap(pick_rows)(jnp.concatenate([grad_expert_in, zero_row], axis=1), places)
    grad_home = lax.all_to_all(
        grad_back.reshape(local_experts, owner_count, slot_depth, width),
        EXPERT,
        split_axis=1,
        concat_axis=1,
        tiled=True,
    )
    grad_home_pad = jnp.concatenate(
        [grad_home.reshape(buffer_rows, width), jnp.zeros((1, width), jnp.bfloat16)], axis=0
    )
    grad_u3 = jnp.sum(
        grad_home_pad[target].reshape(row_count, TOP, width).astype(jnp.float32), axis=1
    )
    expert_shares = (
        lax.psum_scatter(
            grad_expert_up.astype(jnp.bfloat16), DP, scatter_dimension=1, tiled=True
        ).astype(jnp.float32),
        lax.psum_scatter(
            grad_expert_down.astype(jnp.bfloat16), DP, scatter_dimension=1, tiled=True
        ).astype(jnp.float32),
    )
    grad_pick = jnp.sum(grad_out[:, None, :] * y_pair, axis=2)
    grad_gates = jnp.sum(jnp.where(pair_hit, grad_pick[:, :, None], 0.0), axis=1)
    grad_logits = (
        gates * (grad_gates - jnp.sum(gates * grad_gates, axis=1, keepdims=True))
    ).astype(jnp.bfloat16)
    grad_router = jnp.einsum("rd,re->de", u3_low, grad_logits, preferred_element_type=jnp.float32)
    grad_u3 = grad_u3 + jnp.einsum(
        "re,de->rd", grad_logits, w_router, preferred_element_type=jnp.float32
    )
    grad_x2_norm, grad_ln3_gain, grad_ln3_bias = norm_backward(grad_u3, normed3, inverse3, ln3_gain)
    grad_x2 = grad_out + grad_x2_norm
    grad_m = grad_x2.astype(jnp.bfloat16)
    grad_down = jnp.einsum("rf,rd->fd", active2, grad_m, preferred_element_type=jnp.float32)
    grad_active2 = jnp.einsum("rd,fd->rf", grad_m, w_down, preferred_element_type=jnp.float32)
    grad_hidden2 = gelu_pull(hidden2, grad_active2).astype(jnp.bfloat16)
    grad_up = jnp.einsum("rd,rf->df", u2_low, grad_hidden2, preferred_element_type=jnp.float32)
    grad_u2 = jnp.einsum("rf,df->rd", grad_hidden2, w_up, preferred_element_type=jnp.float32)
    grad_x1_norm, grad_ln2_gain, grad_ln2_bias = norm_backward(grad_u2, normed2, inverse2, ln2_gain)
    grad_x1 = grad_x2 + grad_x1_norm
    grad_o = grad_x1.astype(jnp.bfloat16)
    grad_attn_out = jnp.einsum("rd,re->de", mixed_low, grad_o, preferred_element_type=jnp.float32)
    grad_mixed = jnp.einsum(
        "re,de->rd", grad_o, w_attn_out, preferred_element_type=jnp.float32
    ).astype(jnp.bfloat16)
    grad_mixed_seq = grad_mixed.reshape(seq_count, SEQ, HEADS, HD)
    seq_index = 0
    grad_q, grad_k, grad_v = attend_backward(
        qkv_seq[seq_index, :, 0],
        qkv_seq[seq_index, :, 1],
        qkv_seq[seq_index, :, 2],
        seg_seq[seq_index],
        lse_parts[seq_index],
        grad_mixed_seq[seq_index],
    )
    grad_parts = jnp.stack([grad_q, grad_k, grad_v], axis=1)
    grad_qkv_low = grad_parts.reshape(row_count, 3 * width).astype(jnp.bfloat16)
    grad_qkv = jnp.einsum("rd,re->de", u1_low, grad_qkv_low, preferred_element_type=jnp.float32)
    grad_u1 = jnp.einsum("re,de->rd", grad_qkv_low, w_qkv, preferred_element_type=jnp.float32)
    grad_x0_norm, grad_ln1_gain, grad_ln1_bias = norm_backward(grad_u1, normed1, inverse1, ln1_gain)
    grad_tokens = grad_x1 + grad_x0_norm
    dense_parts = (
        lax.psum_scatter(
            grad_qkv.astype(jnp.bfloat16), EXPERT, scatter_dimension=0, tiled=True
        ).astype(jnp.float32),
        lax.psum_scatter(
            grad_attn_out.astype(jnp.bfloat16), EXPERT, scatter_dimension=0, tiled=True
        ).astype(jnp.float32),
        lax.psum_scatter(
            grad_up.astype(jnp.bfloat16), EXPERT, scatter_dimension=0, tiled=True
        ).astype(jnp.float32),
        lax.psum_scatter(
            grad_down.astype(jnp.bfloat16), EXPERT, scatter_dimension=0, tiled=True
        ).astype(jnp.float32),
        lax.psum_scatter(
            grad_router.astype(jnp.bfloat16), EXPERT, scatter_dimension=0, tiled=True
        ).astype(jnp.float32),
        lax.psum_scatter(
            grad_ln1_gain.astype(jnp.bfloat16), EXPERT, scatter_dimension=0, tiled=True
        ).astype(jnp.float32),
        lax.psum_scatter(
            grad_ln1_bias.astype(jnp.bfloat16), EXPERT, scatter_dimension=0, tiled=True
        ).astype(jnp.float32),
        lax.psum_scatter(
            grad_ln2_gain.astype(jnp.bfloat16), EXPERT, scatter_dimension=0, tiled=True
        ).astype(jnp.float32),
        lax.psum_scatter(
            grad_ln2_bias.astype(jnp.bfloat16), EXPERT, scatter_dimension=0, tiled=True
        ).astype(jnp.float32),
        lax.psum_scatter(
            grad_ln3_gain.astype(jnp.bfloat16), EXPERT, scatter_dimension=0, tiled=True
        ).astype(jnp.float32),
        lax.psum_scatter(
            grad_ln3_bias.astype(jnp.bfloat16), EXPERT, scatter_dimension=0, tiled=True
        ).astype(jnp.float32),
        lax.psum_scatter(
            counts.astype(jnp.bfloat16), EXPERT, scatter_dimension=0, tiled=True
        ).astype(jnp.float32),
    )
    dense_sums = (
        lax.psum(dense_parts[0].astype(jnp.bfloat16), DP).astype(jnp.float32),
        lax.psum(dense_parts[1].astype(jnp.bfloat16), DP).astype(jnp.float32),
        lax.psum(dense_parts[2].astype(jnp.bfloat16), DP).astype(jnp.float32),
        lax.psum(dense_parts[3].astype(jnp.bfloat16), DP).astype(jnp.float32),
        lax.psum(dense_parts[4].astype(jnp.bfloat16), DP).astype(jnp.float32),
        lax.psum(dense_parts[5].astype(jnp.bfloat16), DP).astype(jnp.float32),
        lax.psum(dense_parts[6].astype(jnp.bfloat16), DP).astype(jnp.float32),
        lax.psum(dense_parts[7].astype(jnp.bfloat16), DP).astype(jnp.float32),
        lax.psum(dense_parts[8].astype(jnp.bfloat16), DP).astype(jnp.float32),
        lax.psum(dense_parts[9].astype(jnp.bfloat16), DP).astype(jnp.float32),
        lax.psum(dense_parts[10].astype(jnp.bfloat16), DP).astype(jnp.float32),
        lax.psum(dense_parts[11].astype(jnp.bfloat16), DP).astype(jnp.float32),
    )
    (
        sum_qkv,
        sum_attn_out,
        sum_up,
        sum_down,
        sum_router,
        sum_g1,
        sum_b1,
        sum_g2,
        sum_b2,
        sum_g3,
        sum_b3,
        sum_counts,
    ) = dense_sums
    share_up, share_down = expert_shares
    return (
        output,
        grad_tokens,
        sum_g1,
        sum_b1,
        sum_qkv,
        sum_attn_out,
        sum_g2,
        sum_b2,
        sum_up,
        sum_down,
        sum_g3,
        sum_b3,
        sum_router,
        share_up,
        share_down,
        sum_counts,
    )


def mm(a, b):
    return lax.dot_general(a, b, (((1,), (0,)), ((), ())), preferred_element_type=F32)


def mm_nt(a, b):
    return lax.dot_general(a, b, (((1,), (1,)), ((), ())), preferred_element_type=F32)


def mm_tn(a, b):
    return lax.dot_general(a, b, (((0,), (0,)), ((), ())), preferred_element_type=F32)


def row_mean(v):
    return jnp.sum(v, axis=1, keepdims=True) * (1.0 / v.shape[1])


def norm_parts(v):
    centre = v - row_mean(v)
    inverse = lax.rsqrt(row_mean(centre * centre) + epsilon)
    return centre * inverse, inverse


def norm_back(v, du, gain):
    normed, inverse = norm_parts(v)
    dn = du * gain
    inner = dn - row_mean(dn) - normed * row_mean(dn * normed)
    return (
        inverse * inner,
        jnp.sum(du * normed, axis=0, keepdims=True),
        jnp.sum(du, axis=0, keepdims=True),
    )


def gelu_both(h):
    sq = h * h
    t = jnp.tanh(h * (GELU_C + GELU_C * GELU_A * sq))
    u = 0.5 + 0.5 * t
    act = h * u
    slope = u + act * (1.0 - t) * (GELU_C + 3.0 * GELU_C * GELU_A * sq)
    return act, slope


def tile(i, size):
    return pl.ds(pl.multiple_of(i * size, size), size)


NAMES_IN = ["tok", "cot", "ids", "ranks", "seg", "g1", "b1", "g2", "b2", "g3", "b3", "wr"]
NAMES_IN += ["wqkv_h", "wo_h", "wup_h", "wdn_h", "eup_h", "edn_h"]
NAMES_OUT = ["out", "gtok", "small", "gdn", "gup", "go", "gqkv", "geup", "gedn"]
DOWN, UP, ATTN, QKV = range(4)

START, TILE = 35.0, 2.3
FEED, STEP, LAG, HOP, WINDOW = 41.9, 5.8, 8.0, 7.0, 4
AFTER_EXPERTS, BEFORE_BACK, AFTER_NORM, AFTER_MLP = 57.0, 66.0, 75.0, 80.0
AFTER_MLP_GRADS, AFTER_OUT, PAIR_TIME = 84.0, 88.0, 2.5
LINE = 104.0


class Named:
    def __init__(self, pairs):
        self.__dict__.update(pairs)


def make_kernel(
    rows, width, ff, local, experts_all, nx, ng, capacity, room, depth, scratch_names
):
    nz = ng // 2
    steps = nz
    ft = ff // steps
    half = rows // 2
    ep = max(16, experts_all)
    fb, wb = ff // ng, width // ng
    far_first = sorted(range(nz), key=lambda d: (-abs(2 * d - nz + 1), -d))

    def kernel(*refs):
        r = Named(zip(NAMES_IN + NAMES_OUT + scratch_names, refs))
        r.du = r.acc_a.at[pl.ds(0, rows), :]
        r.dx = r.acc_b.at[pl.ds(0, rows), :]
        r.low = r.dyr.at[pl.ds(0, rows), :]
        r.trans = r.xrt.at[:, pl.ds(0, rows)]
        me = lax.axis_index(EXPERT)
        dp = lax.axis_index(DP)
        z, core = dp // 2, lax.rem(dp, 2)
        mate = z * 2 + 1 - core

        across = me + 1 - 2 * lax.rem(me, 2)
        beside = lax.rem(me + 2, nx)

        def peer(k):
            return (me, across, beside, nx - 1 - me)[k]

        loads = [
            pltpu.make_async_copy(src, dst, r.load_sem.at[i])
            for i, (src, dst) in enumerate(
                (
                    (r.tok, r.tokv),
                    (r.wqkv_h, r.wqkv),
                    (r.wo_h, r.wo),
                    (r.wup_h, r.wup),
                    (r.wdn_h, r.wdn),
                    (r.eup_h, r.eup),
                    (r.edn_h, r.edn),
                )
            )
        ]
        loads[0].start()
        loads[1].start()
        own_dz = pltpu.make_async_copy(r.cot, r.dz, r.load_sem.at[7])
        own_dz.start()

        barrier = pltpu.get_barrier_semaphore()
        for k in range(1, nx):
            pl.semaphore_signal(
                barrier, inc=1, device_id={EXPERT: peer(k)}, device_id_type=MESH
            )
        for k in range(1, ng):
            pl.semaphore_signal(
                barrier, inc=1, device_id={DP: lax.rem(dp + k, ng)}, device_id_type=MESH
            )
        pl.semaphore_wait(barrier, nx - 1 + ng - 1)

        def to_expert(src, dst, send, receive, k):
            return pltpu.make_async_remote_copy(
                src_ref=src,
                dst_ref=dst,
                send_sem=send,
                recv_sem=receive,
                device_id={EXPERT: peer(k)},
                device_id_type=MESH,
            )

        def to_dp(src, dst, send, receive, target):
            return pltpu.make_async_remote_copy(
                src_ref=src,
                dst_ref=dst,
                send_sem=send,
                recv_sem=receive,
                device_id={DP: target},
                device_id_type=MESH,
            )

        def direct(src, dst, group, k):
            return to_expert(src, dst, r.send_sem.at[group, k], r.recv_sem.at[group, k], k)

        def rank_copy(k, slot):
            return direct(r.sp_out.at[peer(k)], r.sp_in.at[slot], 0, k)

        def gt_copy(k, slot):
            return direct(r.gt_out.at[peer(k)], r.gt_in.at[slot], 1, k)

        def row_copy(flow, l, k, slot):
            source, target = ((r.out_u, r.in_u), (r.out_z, r.in_z))[flow % 2]
            if flow >= 2:
                source, target = target, source
            at = (flow * local + l) * nx + k
            return to_expert(
                source.at[peer(k), l],
                target.at[slot, l],
                r.row_send.at[at],
                r.row_recv.at[at],
                k,
            )

        line_id = lax.broadcasted_iota(jnp.int32, (8 * nx, 1), 0)
        line_id = jnp.where(
            (line_id & 7) < local, (line_id >> 3) * local + (line_id & 7), -1
        )
        tab = jnp.full((8 * nx, rows), -1, jnp.int32)
        for k in range(r.ids.shape[0]):
            tab = jnp.where(r.ids[k : k + 1, :] == line_id, r.ranks[k : k + 1, :], tab)
        tab = tab.astype(F32)
        earlier = lax.broadcasted_iota(jnp.int32, (rows, rows), 0)
        earlier = jnp.where(earlier < lax.broadcasted_iota(jnp.int32, (rows, rows), 1), 1.0, 0.0)
        named = jnp.where(tab >= 0.0, 1.0, 0.0).astype(BF16)
        slots = jnp.where(tab >= 0.0, mm(named, earlier.astype(BF16)), -1.0)
        level = tab + 1.0
        high = jnp.floor(level * (1.0 / 128.0))
        low = level - 128.0 * high
        slot_id = lax.broadcasted_iota(jnp.int32, (depth, rows), 0).astype(F32)
        for j in range(nx):
            parts = jnp.concatenate(
                [high[8 * j : 8 * j + 8], low[8 * j : 8 * j + 8]], axis=0
            ).astype(BF16)
            r.sp_out[j] = jnp.full((8, depth), -1.0, F32)
            for l in range(local):
                at = 8 * j + l
                r.comp[j, l] = jnp.where(slot_id == slots[at : at + 1], 1.0, 0.0).astype(BF16)
                got = mm_nt(parts, r.comp[j, l])
                r.sp_out[j, l : l + 1, :] = 128.0 * got[l : l + 1] + got[8 + l : 9 + l] - 1.0
        for k in range(1, nx):
            rank_copy(k, me).start()
        r.sp_in[me] = r.sp_out[me]
        own_dz.wait()
        for l in range(local):
            for k in range(1, nx):
                r.out_z[peer(k), l] = mm(r.comp[peer(k), l], r.dz[...]).astype(BF16)
                if l == 0:
                    row_copy(1, l, k, me).start()
            r.in_z[me, l] = mm(r.comp[me, l], r.dz[...]).astype(BF16)
        for copy in loads[2:]:
            copy.start()

        def unit(kind, l, d):
            return (l * 2 + kind) * nz + d

        def block(kind, l, d, side):
            j = d * 2 + side
            if kind == DOWN:
                return r.edn.at[l, pl.ds(pl.multiple_of(j * fb, fb), fb), :]
            return r.eup.at[l, pl.ds(pl.multiple_of(j * wb, wb), wb), :]

        def mate_in(kind, l, d):
            if kind == DOWN:
                return r.xdn.at[l, pl.ds(d * fb, fb), :]
            return r.xup.at[l, pl.ds(d * wb, wb), :]

        def mate_copy(kind, l, d):
            u = unit(kind, l, d)
            return to_dp(
                block(kind, l, d, 1 - core),
                mate_in(kind, l, d),
                r.x_send.at[u],
                r.x_recv.at[u],
                mate,
            )

        def z_slot(kind, l, s):
            return (r.zdn if kind == DOWN else r.zup).at[l, s]

        def right_copy(kind, l, d):
            u = unit(kind, l, d)
            return to_dp(
                block(kind, l, d, core),
                z_slot(kind, l, d + 1),
                r.z_send.at[u],
                r.z_recv.at[u, 0],
                lax.rem(dp + 2, ng),
            )

        def left_copy(kind, l, d):
            u = unit(kind, l, d)
            return to_dp(
                block(kind, l, d, core),
                z_slot(kind, l, d),
                r.z_send.at[u],
                r.z_recv.at[u, 1],
                lax.rem(dp + ng - 2, ng),
            )

        def add_to(ref, other):
            ref[...] = (ref[...].astype(F32) + other[...].astype(F32)).astype(BF16)

        waiting, joined = [], set()

        def ready(m):
            return all(u in waiting or u in joined for u in (rightward[m], leftward[m]))

        def settle(m):
            while not {rightward[m], leftward[m]} <= joined:
                join(*waiting.pop(0))

        def join(kind, l, d):
            joined.add((kind, l, d))
            mate_copy(kind, l, d).wait_recv()
            add_to(block(kind, l, d, core), mate_in(kind, l, d))

        groups = [(kind, l) for l in range(local) for kind in (DOWN, UP)]
        rightward = [(kind, l, d) for kind, l in groups for d in reversed(range(1, nz))]
        leftward = [(kind, l, d) for kind, l in groups for d in range(nz - 1)]

        def feed(m):
            settle(m)

            @pl.when(z == 0)
            def _():
                if m >= WINDOW:
                    right_copy(*rightward[m - WINDOW]).wait_send()
                right_copy(*rightward[m]).start()

            @pl.when(z == nz - 1)
            def _():
                if m >= WINDOW:
                    left_copy(*leftward[m - WINDOW]).wait_send()
                left_copy(*leftward[m]).start()

        def hop(m, h):
            settle(m)
            right, left = rightward[m], leftward[m]
            if right[2] > h:

                @pl.when(z == h)
                def _():
                    right_copy(*right).wait_recv()
                    add_to(block(*right, core), z_slot(*right[:2], right[2] + 1))
                    right_copy(*right).start()

            if left[2] < nz - 1 - h:

                @pl.when(z == nz - 1 - h)
                def _():
                    left_copy(*left).wait_recv()
                    add_to(block(*left, core), z_slot(*left))
                    left_copy(*left).start()

        def land(kind, l):
            for d in range(nz):

                @pl.when(z == d)
                def _():
                    if d > 0:
                        right_copy(kind, l, d).wait_recv()
                        add_to(block(kind, l, d, core), z_slot(kind, l, d + 1))
                    if d < nz - 1:
                        left_copy(kind, l, d).wait_recv()
                        add_to(block(kind, l, d, core), z_slot(kind, l, d))

        shared = (
            (r.wdn, r.xdn, 0, r.bdn, r.cdn, ff, width),
            (r.wup, r.xup, 0, r.bup, r.cup, width, ff),
            (r.wo, r.xdn, 1, r.bo, r.co, width, width),
            (r.wqkv, r.xup, 1, r.bqkv, r.cqkv, width, 3 * width),
        )

        def sizes(t):
            q = shared[t][5] // nx
            return q, q // 2, q // 2 // nz

        def half_of(t, q, side):
            rq, rh, _ = sizes(t)
            return shared[t][0].at[pl.ds(pl.multiple_of(q * rq + side * rh, rh), rh), :]

        def part_of(t, d, side):
            rq, rh, rz = sizes(t)
            start = pl.multiple_of(me * rq + side * rh + d * rz, rz)
            return shared[t][0].at[pl.ds(start, rz), :]

        def swap_in(t, q):
            _, rh, _ = sizes(t)
            _, buffer, l, _, _, _, wide = shared[t]
            return buffer.at[l, pl.ds(pl.multiple_of(q * rh, rh), rh), pl.ds(0, wide)]

        def swap_copy(t, q):
            return to_dp(
                half_of(t, q, 1 - core),
                swap_in(t, q),
                r.a_send.at[t, q],
                r.a_recv.at[t, q],
                mate,
            )

        def quarter(t, k, c):
            rq, rh, _ = sizes(t)
            start = pl.multiple_of(peer(k) * rq + core * rh + c * (rh // 2), rh // 2)
            return shared[t][0].at[pl.ds(start, rh // 2), :]

        def plane_cross(t, c):
            return to_expert(
                quarter(t, 3, c),
                shared[t][3].at[2, c],
                r.b_send.at[t, 4 + c],
                r.b_recv.at[t, 4 + c],
                c + 1,
            )

        def plane_copy(t, k, c):
            at = (k - 1) * 2 + c
            return to_expert(
                quarter(t, k, c),
                shared[t][3].at[k - 1, c],
                r.b_send.at[t, at],
                r.b_recv.at[t, at],
                k,
            )

        done = (
            r.s2.at[pl.ds(0, ff // nx), pl.ds(0, width)],
            r.a2.at[pl.ds(0, width // nx), :],
            r.s2.at[pl.ds(0, width // nx), pl.ds(width, width)],
            r.a2.at[pl.ds(width // nx, width // nx), pl.ds(0, 3 * width)],
        )

        def done_part(t, d, side):
            _, rh, rz = sizes(t)
            return done[t].at[pl.ds(pl.multiple_of(side * rh + d * rz, rz), rz), :]

        def give_copy(t, k, d, side):
            part = done_part(t, d, side)
            return to_dp(part, part, r.p_send.at[t, k], r.p_recv.at[t, k], mate)

        def near_copy(t, k):
            return to_dp(
                part_of(t, lax.rem(z + k, nz), core),
                shared[t][4].at[k],
                r.c_send.at[t, k],
                r.c_recv.at[t, k],
                lax.rem(dp + 2 * k, ng),
            )

        def far_copy(t, k, d):
            part = done_part(t, d, core)
            send, receive = r.n_send.at[t, k], r.n_recv.at[t, k]
            return to_dp(part, part, send, receive, lax.rem(dp + 2 * k, ng))

        def near_join(t):
            total = part_of(t, z, core)[...].astype(F32)
            for k in range(1, nz):
                near_copy(t, k).wait_recv()
                total += shared[t][4][k].astype(F32)
            done_part(t, z, core)[...] = total.astype(BF16)
            for k in range(1, nz):
                far_copy(t, k, z).start()
            give_copy(t, 0, z, core).start()

        def far_join(t):
            for k in range(1, nz):
                d = lax.rem(z + nz - k, nz)
                far_copy(t, k, d).wait_recv()
                give_copy(t, k, d, core).start()

        def swap(t):
            for q in range(nx):
                swap_copy(t, q).start()

        def plane_one(t):
            for k in (3, 1, 2, 0):
                q = peer(k)
                swap_copy(t, q).wait_recv()
                add_to(half_of(t, q, core), swap_in(t, q))
                if k == 3:
                    for c in range(2):
                        plane_cross(t, c).start()

        def plane_two(t):
            for c in range(2):
                plane_cross(t, c).wait_recv()
                add_to(quarter(t, 2 - c, c), shared[t][3].at[2, c])
            for c in range(2):
                for k in (1, 2):
                    plane_copy(t, k, c).start()

        def line_start(t):
            for c in range(2):
                for k in (1, 2):
                    plane_copy(t, k, c).wait_recv()
                mine = quarter(t, 0, c)
                total = mine[...].astype(F32)
                for k in (1, 2):
                    total += shared[t][3][k - 1, c].astype(F32)
                mine[...] = total.astype(BF16)
            for k in range(1, nz):
                near_copy(t, k).start()

        loads[0].wait()
        for c in range(2):
            span = pl.ds(c * half, half)
            normed, _ = norm_parts(r.tokv[span, :].astype(F32))
            r.u1[span, :] = (normed * r.g1[...] + r.b1[...]).astype(BF16)
        loads[1].wait()
        for i in range(3):
            part = mm(r.u1[...], r.wqkv[:, i * width : (i + 1) * width]).astype(BF16)
            r.qkv[i] = part * jnp.asarray(0.125, BF16) if i == 0 else part
        seg_row = jnp.broadcast_to(r.seg[...].astype(F32), (8, rows))
        seg_col = jnp.transpose(seg_row)[:, 0:1]
        r.du[...] = jnp.where(seg_col == seg_row[0:1, :], 0.0, -1e30)
        lane = lax.broadcasted_iota(jnp.int32, (1, PAIR), 1)
        masks = (
            jnp.where(lane < HD, 1.0, 0.0).astype(BF16),
            jnp.where(lane < HD, 0.0, 1.0).astype(BF16),
        )

        @pl.loop(0, width // PAIR)
        def _(pair):
            cols = tile(pair, PAIR)
            keys, values = r.qkv[1, :, cols], r.qkv[2, :, cols]
            for c in range(2):
                span = pl.ds(c * half, half)
                queries = r.qkv[0, span, cols]
                mixed = jnp.zeros((half, PAIR), F32)
                for h in range(2):
                    s = mm_nt(queries * masks[h], keys) + r.du[span, :]
                    e = jnp.exp(s - jnp.max(s, axis=1, keepdims=True))
                    p = (e * (1.0 / jnp.sum(e, axis=1, keepdims=True))).astype(BF16)
                    r.probs[pair * 2 + h, span, :] = p
                    mixed += mm(p, values * masks[h])
                r.ao[span, cols] = mixed.astype(BF16)

        for l in range(1, local):
            for k in range(1, nx):
                row_copy(1, l - 1, k, me).wait_send()
                row_copy(1, l, k, me).start()
        for i in (2, 3, 4):
            loads[i].wait()
        for c in range(2):
            span = pl.ds(c * half, half)
            x1 = r.tokv[span, :].astype(F32) + mm(r.ao[span, :], r.wo[...])
            r.x1[span, :] = x1
            normed, _ = norm_parts(x1)
            r.u2[span, :] = (normed * r.g2[...] + r.b2[...]).astype(BF16)
            r.x2[span, :] = x1

            @pl.loop(0, steps)
            def _(t):
                cols = tile(t, ft)
                act, slope = gelu_both(mm(r.u2[span, :], r.wup[:, cols]))
                act = act.astype(BF16)
                r.a2[span, cols] = act
                r.s2[span, cols] = slope.astype(BF16)
                r.x2[span, :] += mm(act, r.wdn[cols, :])

            normed, _ = norm_parts(r.x2[span, :])
            r.u3[span, :] = (normed * r.g3[...] + r.b3[...]).astype(BF16)

        def compact(l):
            for k in range(1, nx):
                r.out_u[peer(k), l] = mm(r.comp[peer(k), l], r.u3[...]).astype(BF16)
                if l == 0:
                    row_copy(0, l, k, me).start()
            r.in_u[me, l] = mm(r.comp[me, l], r.u3[...]).astype(BF16)

        for l in range(local):
            compact(l)
        for k in range(1, nx):
            rank_copy(k, peer(k)).wait_recv()
        r.small2[...] = jnp.zeros(r.small2.shape, F32)
        for l in range(local):
            routed = jnp.zeros((1, depth), F32)
            for j in range(nx):
                routed += jnp.where(r.sp_in[j, l : l + 1, :] >= 0.0, 1.0, 0.0)
            routed = jnp.sum(routed, axis=1, keepdims=True)
            kept = jnp.minimum(routed, float(capacity))
            spot = lax.broadcasted_iota(jnp.int32, (1, r.small2.shape[1]), 1)
            line = jnp.where(spot == 0, kept, jnp.where(spot == 1, routed - kept, 0.0))
            r.small2[8 + ep + l : 9 + ep + l, :] = line
        columns = [jnp.transpose(r.sp_in[j]) for j in range(nx)]
        for j in range(nx):
            r.rank[j] = jnp.full((8, depth), -1.0, F32)
            for l in range(local):
                mine = r.sp_in[j, l : l + 1, :]
                above = jnp.zeros((1, depth), F32)
                for column in columns:
                    above += jnp.sum(
                        jnp.where(column[:, l : l + 1] > mine, 1.0, 0.0), axis=0, keepdims=True
                    )
                keep = (mine >= 0.0) & (above < float(capacity))
                r.rank[j, l : l + 1, :] = jnp.where(keep, above, -1.0)

        row_id = lax.broadcasted_iota(jnp.int32, (room, depth), 0).astype(F32)

        def gather(source, target, l):
            total = jnp.zeros((room, width), F32)
            for j in range(nx):
                pick = jnp.where(row_id == r.rank[j, l : l + 1, :], 1.0, 0.0).astype(BF16)
                total += mm(pick, source[j, l])
            target[l] = total.astype(BF16)

        def fetch(l):
            for k in range(1, nx):
                row_copy(1, l, k, peer(k)).wait_recv()
            gather(r.in_z, r.dzr, l)
            for k in range(1, nx):
                row_copy(0, l, k, peer(k)).wait_recv()
            gather(r.in_u, r.xr, l)

        for k in range(1, nx):
            row_copy(1, local - 1, k, me).wait_send()
        for l in range(1, local):
            for k in range(1, nx):
                row_copy(0, l - 1, k, me).wait_send()
                row_copy(0, l, k, me).start()
        fetch(0)

        loads[5].wait()
        loads[6].wait()
        lane_e = lax.broadcasted_iota(jnp.int32, (room, ep), 1)
        router = r.wr[...].astype(F32)
        if ep > experts_all:
            spare = jnp.zeros((ep - experts_all, width), F32)
            router = jnp.concatenate([router, spare], axis=0)
        r.wrt[...] = router.astype(BF16)
        lane_id = lax.broadcasted_iota(jnp.int32, (depth, room), 1).astype(F32)

        def spread(j, l, found):
            ranks = jnp.transpose(r.rank[j])[:, l : l + 1]
            put = jnp.where(lane_id == ranks, 1.0, 0.0).astype(BF16)
            return mm(put, found[l]).astype(BF16)

        def send_rows(flow, l):
            found, source, target = ((r.xr, r.in_u, r.out_u), (r.dzr, r.in_z, r.out_z))[flow % 2]
            for k in range(1, nx):
                source[peer(k), l] = spread(peer(k), l, found)
                if flow == 3:
                    row_copy(flow, l, k, me).start()
            target[me, l] = spread(me, l, found)

        def gate_grads(j):
            r.gt_out[j] = jnp.zeros((8, depth), F32)
            for l in range(local):
                hit = row_id == r.rank[j, l : l + 1, :]
                line = jnp.sum(jnp.where(hit, r.dgate[l], 0.0), axis=0, keepdims=True)
                r.gt_out[j, l : l + 1, :] = line

        events = []
        for m in range(len(rightward)):
            events.append((FEED + STEP * max(0, m - WINDOW + 2), m, functools.partial(feed, m)))
            for h in range(1, nz - 1):
                arrival = FEED + STEP * (m + 1) + LAG + HOP * (h - 1)
                events.append((arrival, m, functools.partial(hop, m, h)))
        events.sort(key=lambda event: event[0])

        def pump(now):
            while events and events[0][0] <= now and (events[0][1] < 0 or ready(events[0][1])):
                events.pop(0)[2]()

        clock = START
        for l in range(local):
            if l:
                fetch(l)
            rows_in = r.xr[l]
            r.xrt[...] = jnp.transpose(rows_in)
            logits = jnp.where(lane_e < experts_all, mm_nt(rows_in, r.wrt[...]), -1e30)
            e = jnp.exp(logits - jnp.max(logits, axis=1, keepdims=True))
            gate = jnp.sum(
                jnp.where(lane_e == me * local + l, e, 0.0), axis=1, keepdims=True
            ) / jnp.sum(e, axis=1, keepdims=True)
            r.dyr[...] = (r.dzr[l].astype(F32) * gate).astype(BF16)
            for i, d in enumerate(far_first):
                cols = pl.ds(d * ft, ft)
                for c in range(2):
                    side = pl.ds(c * (ft // 2), ft // 2)
                    part = pl.ds(d * ft + c * (ft // 2), ft // 2)
                    act, slope = gelu_both(mm(r.xr[l], r.eup[l, :, part]))
                    r.act[:, side] = act.astype(BF16)
                    r.dh[:, side] = (mm_nt(r.dyr[...], r.edn[l, part, :]) * slope).astype(BF16)
                y = mm(r.act[...], r.edn[l, cols, :])
                dx = mm_nt(r.dh[...], r.eup[l, :, cols])
                if i:
                    r.acc_a[...] += y
                    r.acc_b[...] += dx
                else:
                    r.acc_a[...] = y
                    r.acc_b[...] = dx
                r.edn[l, cols, :] = mm_tn(r.act[...], r.dyr[...]).astype(BF16)
                r.eup[l, :, cols] = mm(r.xrt[...], r.dh[...]).astype(BF16)
                mate_copy(DOWN, l, d).start()
                for _ in range(1 + l):
                    if waiting:
                        join(*waiting.pop(0))
                waiting.append((DOWN, l, d))
                clock += TILE
                pump(clock)
            for d in far_first:
                mate_copy(UP, l, d).start()
                waiting.append((UP, l, d))
            y = r.acc_a[...].astype(BF16).astype(F32)
            r.dgate[l] = jnp.sum(r.dzr[l].astype(F32) * y, axis=1, keepdims=True)
            r.xr[l] = (y * gate).astype(BF16)
            r.dzr[l] = r.acc_b[...].astype(BF16)
            if l == 0:
                for k in range(1, nx):
                    row_copy(0, local - 1, k, me).wait_send()
            send_rows(3, l)
            pump(clock + 1.0)

        while waiting:
            join(*waiting.pop(0))
        pl.semaphore_signal(r.credit, inc=1, device_id={DP: mate}, device_id_type=MESH)
        for k in range(1, nx):
            gate_grads(peer(k))
            gt_copy(k, me).start()
        gate_grads(me)
        r.gt_in[me] = r.gt_out[me]
        pump(AFTER_EXPERTS)
        for l in range(local):
            send_rows(2, l)
        pump(BEFORE_BACK)

        for k in range(1, nx):
            gt_copy(k, peer(k)).wait_recv()
        r.gt_sum[...] = jnp.zeros((ep, rows), F32)
        for j in range(nx):
            column = jnp.transpose(r.gt_in[j])
            for l in range(local):
                spots = r.comp[j, l].astype(F32) * column[:, l : l + 1]
                line = jnp.sum(spots, axis=0, keepdims=True)
                r.gt_sum[j * local + l : j * local + l + 1, :] = line
        dgates = r.gt_sum[...]
        for l in range(local):
            for k in range(1, nx):
                row_copy(3, l, k, peer(k)).wait_recv()
        def at_home(source, c):
            chosen = jnp.concatenate(
                [r.comp[j, l, :, pl.ds(c * half, half)] for j in range(nx) for l in range(local)],
                axis=0,
            )
            found = jnp.concatenate(
                [source[j, l] for j in range(nx) for l in range(local)], axis=0
            )
            return mm_tn(chosen, found)

        row_e = lax.broadcasted_iota(jnp.int32, (ep, rows), 0)
        u3 = r.u3[...]
        logits = jnp.where(row_e < experts_all, mm_nt(r.wrt[...], u3), -1e30)
        e = jnp.exp(logits - jnp.max(logits, axis=0, keepdims=True))
        gates = e / jnp.sum(e, axis=0, keepdims=True)
        dlogits = (
            gates * (dgates - jnp.sum(gates * dgates, axis=0, keepdims=True))
        ).astype(BF16)
        r.small1[8 : 8 + ep, :] = mm(dlogits, u3)
        for c in range(2):
            span = pl.ds(c * half, half)
            r.du[span, :] = at_home(r.out_z, c) + mm_tn(
                dlogits[:, c * half : (c + 1) * half], r.wrt[...]
            )

        def norm_step(value, gain, base, line, pieces=2):
            size = rows // pieces

            def one(i, sums):
                span = tile(i, size)
                dv, dgain, dbias = norm_back(
                    value[span, :].astype(F32), r.du[span, :], gain[...]
                )
                r.dx[span, :] = base(span) + dv
                return sums[0] + dgain, sums[1] + dbias

            zero = jnp.zeros((1, width), F32)
            dgain, dbias = lax.fori_loop(0, pieces, one, (zero, zero))
            r.small1[line : line + 1, :] = dgain
            r.small1[line + 1 : line + 2, :] = dbias

        r.small1[0:8, :] = jnp.zeros((8, width), F32)
        norm_step(r.x2, r.g3, lambda span: r.dz[span, :].astype(F32), 4)
        r.low[...] = r.dx[...].astype(BF16)
        r.trans[...] = jnp.transpose(r.u2[...])
        r.du[...] = jnp.zeros((rows, width), F32)

        pump(AFTER_NORM)

        @pl.loop(0, steps)
        def _(t):
            cols = tile(t, ft)
            dm = r.low[...]
            dh = (mm_nt(dm, r.wdn[cols, :]) * r.s2[:, cols].astype(F32)).astype(BF16)
            r.s2[:, cols] = dh
            r.du[...] += mm_nt(dh, r.wup[:, cols])

        pump(AFTER_MLP)

        @pl.loop(0, steps)
        def _(t):
            cols = tile(t, ft)
            r.wdn[cols, :] = mm_tn(r.a2[:, cols], r.low[...]).astype(BF16)

        pl.semaphore_wait(r.credit, 1)
        swap(DOWN)

        @pl.loop(0, steps)
        def _(t):
            cols = tile(t, ft)
            r.wup[:, cols] = mm(r.trans[...], r.s2[:, cols]).astype(BF16)

        swap(UP)
        plane_one(DOWN)
        pump(AFTER_MLP_GRADS)
        norm_step(r.x1, r.g2, lambda span: r.dx[span, :], 2)
        do = r.dx[...].astype(BF16)
        r.low[...] = mm_nt(do, r.wo[...]).astype(BF16)
        r.wo[...] = mm_tn(r.ao[...], do).astype(BF16)
        swap(ATTN)
        plane_one(UP)
        pump(AFTER_OUT)

        for pair in range(width // PAIR):
            cols = pl.ds(pair * PAIR, PAIR)
            keys, values = r.qkv[1, :, cols], r.qkv[2, :, cols]
            dk = jnp.zeros((rows, PAIR), F32)
            dv = jnp.zeros((rows, PAIR), F32)
            for c in range(2):
                span = pl.ds(c * half, half)
                queries = r.qkv[0, span, cols]
                dao = r.low[span, cols]
                dq = jnp.zeros((half, PAIR), F32)
                for h in range(2):
                    p = r.probs[pair * 2 + h, span, :]
                    mine = dao * masks[h]
                    weighed = p.astype(F32) * mm_nt(mine, values)
                    total = jnp.sum(weighed, axis=1, keepdims=True)
                    ds = (weighed - p.astype(F32) * total).astype(BF16)
                    dq += mm(ds, keys * masks[h])
                    dk += mm_tn(ds, queries * masks[h])
                    dv += mm_tn(p, mine)
                r.qkv[0, span, cols] = (dq * 0.125).astype(BF16)
            r.qkv[1, :, cols] = dk.astype(BF16)
            r.qkv[2, :, cols] = dv.astype(BF16)
            if pair == 0:
                plane_two(DOWN)
            if pair == 1:
                plane_two(UP)
                plane_one(ATTN)
            if pair == 2:
                plane_two(ATTN)
            if pair == 3:
                line_start(DOWN)
            pump(AFTER_OUT + PAIR_TIME * (pair + 1))

        r.trans[...] = jnp.transpose(r.u1[...])
        du = jnp.zeros((rows, width), F32)
        for i in range(3):
            cols = slice(i * width, (i + 1) * width)
            du += mm_nt(r.qkv[i], r.wqkv[:, cols])
            r.wqkv[:, cols] = mm(r.trans[...], r.qkv[i]).astype(BF16)
        swap(QKV)
        r.du[...] = du
        norm_step(r.tokv, r.g1, lambda span: r.dx[span, :], 0)
        early = [pltpu.make_async_copy(r.dx, r.gtok, r.load_sem.at[8])]
        early[0].start()
        plane_one(QKV)
        line_start(UP)
        line_start(ATTN)

        wide = width // nx

        def small_copy(k, slot):
            start = pl.multiple_of(peer(k) * wide, wide)
            return direct(r.small1.at[:, pl.ds(start, wide)], r.s1_in.at[slot], 2, k)

        for k in range(1, nx):
            small_copy(k, me).start()

        def start_y():
            for l in range(local):
                for k in range(1, nx):
                    row_copy(2, l, k, me).start()

        def finish_y():
            for l in range(local):
                for k in range(1, nx):
                    row_copy(2, l, k, peer(k)).wait_recv()
            for c in range(2):
                span = pl.ds(c * half, half)
                r.u3[span, :] = (r.x2[span, :] + at_home(r.out_u, c)).astype(BF16)
            early.append(pltpu.make_async_copy(r.u3, r.out, r.load_sem.at[9]))
            early[1].start()


        def small_join():
            for k in range(1, nx):
                small_copy(k, peer(k)).wait_recv()
            total = r.small1[:, pl.ds(pl.multiple_of(me * wide, wide), wide)]
            for k in range(1, nx):
                total += r.s1_in[peer(k)]
            r.small2[0 : 8 + ep, :] = total

        def small2_copy(k, slot):
            return to_dp(
                r.small2,
                r.s2_in.at[slot],
                r.s_send.at[k],
                r.s_recv.at[k],
                lax.rem(dp + k, ng),
            )

        def small_send():
            small_join()
            for k in range(1, ng):
                small2_copy(k, dp).start()
            r.s2_in[dp] = r.small2[...]


        def later(offset, step, *args):
            events.append((LINE + offset, -1, functools.partial(step, *args)))

        later(3.0, plane_two, QKV)
        later(7.0, line_start, QKV)
        later(7.1, near_join, DOWN)
        later(8.0, near_join, UP)
        later(9.0, near_join, ATTN)
        later(12.0, near_join, QKV)
        for i, t in enumerate((DOWN, UP, ATTN, QKV)):
            later(24.0 + i, far_join, t)
        later(2.5, small_send)
        later(7.0, start_y)
        later(23.0, finish_y)
        for i, (kind, l) in enumerate(groups):
            later(22.0 + 0.1 * i, land, kind, l)
        events.sort(key=lambda event: event[0])
        pump(math.inf)

        for k in range(1, ng):
            small2_copy(k, lax.rem(dp + ng - k, ng)).wait_recv()
        total = r.s2_in[0]
        for j in range(1, ng):
            total += r.s2_in[j]
        r.small[...] = total

        saves = []
        for kind, target in ((DOWN, r.gedn), (UP, r.geup)):
            for l in range(local):
                saves.append((block(kind, l, z, core), target.at[l]))
        for t, target in enumerate((r.gdn, r.gup, r.go, r.gqkv)):
            for k in range(nz):
                give_copy(t, k, lax.rem(z + nz - k, nz), 1 - core).wait_recv()
            saves.append((done[t], target))
        saves = [
            pltpu.make_async_copy(src, dst, r.load_sem.at[i])
            for i, (src, dst) in enumerate(saves)
        ]
        for copy in saves:
            copy.start()
        for copy in saves + early:
            copy.wait()

        for k in range(1, nx):
            rank_copy(k, me).wait_send()
            gt_copy(k, me).wait_send()
            small_copy(k, me).wait_send()
            for l in range(local):
                row_copy(2, l, k, me).wait_send()
                row_copy(3, l, k, me).wait_send()
        for k in range(1, ng):
            small2_copy(k, dp).wait_send()
        for l in range(local):
            for kind in (DOWN, UP):
                for d in range(nz):
                    mate_copy(kind, l, d).wait_send()
        for m, (right, left) in enumerate(zip(rightward, leftward)):
            last = m >= len(rightward) - WINDOW

            @pl.when((z < right[2]) & (last | (z > 0)))
            def _():
                right_copy(*right).wait_send()

            @pl.when((z > left[2]) & (last | (z < nz - 1)))
            def _():
                left_copy(*left).wait_send()

        for t in range(4):
            for q in range(nx):
                swap_copy(t, q).wait_send()
            for c in range(2):
                plane_cross(t, c).wait_send()
                for k in (1, 2):
                    plane_copy(t, k, c).wait_send()
            for k in range(nz):
                give_copy(t, k, z, core).wait_send()
                if k:
                    near_copy(t, k).wait_send()
                    far_copy(t, k, z).wait_send()

    return kernel


def fits(scratch):
    total = 0
    for buffer in scratch.values():
        if buffer.dtype in (F32, BF16):
            lead, (high, wide) = buffer.shape[:-2], buffer.shape[-2:]
            lanes = (wide + 127) // 128 * 128
            total += math.prod(lead) * high * lanes * jnp.dtype(buffer.dtype).itemsize
    return total < VMEM_PLAN


def shards(*args):
    got = kernel_shards(*args)
    return plain_shards(*args) if got is None else got


def kernel_shards(
    tokens,
    segments,
    experts,
    priority,
    cotangent,
    ln1_gain,
    ln1_bias,
    w_qkv,
    w_attn_out,
    ln2_gain,
    ln2_bias,
    w_up,
    w_down,
    ln3_gain,
    ln3_bias,
    w_router,
    expert_up,
    expert_down,
):
    rows, width = tokens.shape
    local, _, ff = expert_up.shape
    experts_all = w_router.shape[1]
    nx, ng = lax.axis_size(EXPERT), lax.axis_size(DP)
    nz = ng // 2
    capacity = (21 * rows + 10 * local - 1) // (10 * local)
    room = (capacity + 15) // 16 * 16
    heads = width // HD
    depth = 3 * rows // experts_all
    ep = max(16, experts_all)
    fb, wb = ff // ng, width // ng
    line = lambda v: v.reshape(1, width)
    hbm = pl.BlockSpec(memory_space=pl.ANY)
    vmem = pl.BlockSpec(memory_space=pltpu.VMEM)
    dma = pltpu.SemaphoreType.DMA
    units = local * 2 * nz

    def by_plane(high, wide):
        return pltpu.VMEM((3, 2, high // nx // 4, wide), BF16)

    def by_line(high, wide):
        return pltpu.VMEM((nz + 1, high // nx // 2 // nz, wide), BF16)

    scratch = dict(
        tokv=pltpu.VMEM((rows, width), BF16),
        wqkv=pltpu.VMEM(w_qkv.shape, BF16),
        wo=pltpu.VMEM(w_attn_out.shape, BF16),
        wup=pltpu.VMEM(w_up.shape, BF16),
        wdn=pltpu.VMEM(w_down.shape, BF16),
        eup=pltpu.VMEM(expert_up.shape, BF16),
        edn=pltpu.VMEM(expert_down.shape, BF16),
        wrt=pltpu.VMEM((ep, width), BF16),
        u1=pltpu.VMEM((rows, width), BF16),
        qkv=pltpu.VMEM((3, rows, width), BF16),
        probs=pltpu.VMEM((heads, rows, rows), BF16),
        ao=pltpu.VMEM((rows, width), BF16),
        x1=pltpu.VMEM((rows, width), F32),
        u2=pltpu.VMEM((rows, width), BF16),
        a2=pltpu.VMEM((rows, ff), BF16),
        s2=pltpu.VMEM((rows, ff), BF16),
        x2=pltpu.VMEM((rows, width), F32),
        u3=pltpu.VMEM((rows, width), BF16),
        dz=pltpu.VMEM((rows, width), BF16),
        comp=pltpu.VMEM((nx, local, depth, rows), BF16),
        out_u=pltpu.VMEM((nx, local, depth, width), BF16),
        in_u=pltpu.VMEM((nx, local, depth, width), BF16),
        out_z=pltpu.VMEM((nx, local, depth, width), BF16),
        in_z=pltpu.VMEM((nx, local, depth, width), BF16),
        sp_out=pltpu.VMEM((nx, 8, depth), F32),
        sp_in=pltpu.VMEM((nx, 8, depth), F32),
        rank=pltpu.VMEM((nx, 8, depth), F32),
        act=pltpu.VMEM((room, ff // nz), BF16),
        dh=pltpu.VMEM((room, ff // nz), BF16),
        acc_a=pltpu.VMEM((room, width), F32),
        acc_b=pltpu.VMEM((room, width), F32),
        xr=pltpu.VMEM((local, room, width), BF16),
        xrt=pltpu.VMEM((width, room), BF16),
        dzr=pltpu.VMEM((local, room, width), BF16),
        dyr=pltpu.VMEM((room, width), BF16),
        dgate=pltpu.VMEM((local, room, 1), F32),
        gt_out=pltpu.VMEM((nx, 8, depth), F32),
        gt_in=pltpu.VMEM((nx, 8, depth), F32),
        gt_sum=pltpu.VMEM((ep, rows), F32),
        small1=pltpu.VMEM((8 + ep, width), F32),
        small2=pltpu.VMEM((16 + ep, width // nx), F32),
        s1_in=pltpu.VMEM((nx, 8 + ep, width // nx), F32),
        s2_in=pltpu.VMEM((ng, 16 + ep, width // nx), F32),
        xdn=pltpu.VMEM((local, ff // 2, width), BF16),
        xup=pltpu.VMEM((local, width // 2, ff), BF16),
        zdn=pltpu.VMEM((local, nz + 1, fb, width), BF16),
        zup=pltpu.VMEM((local, nz + 1, wb, ff), BF16),
        bdn=by_plane(ff, width),
        bup=by_plane(width, ff),
        bo=by_plane(width, width),
        bqkv=by_plane(width, 3 * width),
        cdn=by_line(ff, width),
        cup=by_line(width, ff),
        co=by_line(width, width),
        cqkv=by_line(width, 3 * width),
        credit=pltpu.SemaphoreType.REGULAR,
        load_sem=dma((16,)),
        send_sem=dma((3, nx)),
        recv_sem=dma((3, nx)),
        row_send=dma((4 * local * nx,)),
        row_recv=dma((4 * local * nx,)),
        x_send=dma((units,)),
        x_recv=dma((units,)),
        z_send=dma((units,)),
        z_recv=dma((units, 2)),
        a_send=dma((4, nx)),
        a_recv=dma((4, nx)),
        b_send=dma((4, 6)),
        b_recv=dma((4, 6)),
        c_send=dma((4, nz)),
        c_recv=dma((4, nz)),
        p_send=dma((4, nz)),
        p_recv=dma((4, nz)),
        n_send=dma((4, nz)),
        n_recv=dma((4, nz)),
        s_send=dma((ng,)),
        s_recv=dma((ng,)),
    )
    if nx != 4 or not fits(scratch):
        return None
    sds = jax.ShapeDtypeStruct
    outs = dict(
        out=sds((rows, width), BF16),
        gtok=sds((rows, width), F32),
        small=sds((16 + ep, width // nx), F32),
        gdn=sds((ff // nx, width), BF16),
        gup=sds((width // nx, ff), BF16),
        go=sds((width // nx, width), BF16),
        gqkv=sds((width // nx, 3 * width), BF16),
        geup=sds((local, wb, ff), BF16),
        gedn=sds((local, fb, width), BF16),
    )
    got = pl.pallas_call(
        make_kernel(
            rows, width, ff, local, experts_all, nx, ng, capacity, room, depth, list(scratch)
        ),
        out_shape=tuple(outs[name] for name in NAMES_OUT),
        in_specs=[hbm, hbm] + [vmem] * 10 + [hbm] * 6,
        out_specs=(hbm, hbm, vmem) + (hbm,) * 6,
        scratch_shapes=list(scratch.values()),
        compiler_params=pltpu.CompilerParams(
            collective_id=0, has_side_effects=True, vmem_limit_bytes=63 << 20
        ),
    )(
        tokens,
        cotangent,
        experts.T,
        priority.T,
        segments.reshape(1, rows),
        line(ln1_gain),
        line(ln1_bias),
        line(ln2_gain),
        line(ln2_bias),
        line(ln3_gain),
        line(ln3_bias),
        w_router.T,
        w_qkv,
        w_attn_out,
        w_up,
        w_down,
        expert_up,
        expert_down,
    )
    return finish(got, experts_all, local)


def finish(got, experts_all, local):
    out, gtok, small, *low = got
    wide = small.shape[1]
    ep = max(16, experts_all)

    def kernel(*refs):
        count = len(low)
        out_in, gtok_in, small_in = refs[:3]
        low_in, refs = refs[3 : 3 + count], refs[3 + count :]
        out_to, gtok_to = refs[:2]
        lines, router, counts = refs[2:8], refs[8], refs[9]
        high_out, refs = refs[10 : 10 + count], refs[10 + count :]
        short, long, sem = refs[:count], refs[count : 2 * count], refs[2 * count]
        held = refs[2 * count + 1 :]
        through = [
            pltpu.make_async_copy(out_in, held[0], sem.at[0]),
            pltpu.make_async_copy(gtok_in, held[1], sem.at[1]),
        ]
        loads = [
            pltpu.make_async_copy(low_in[i], short[i], sem.at[2 + i]) for i in range(count)
        ]
        for copy in loads + through:
            copy.start()
        copies = []
        for i in range(6):
            lines[i][...] = small_in[i : i + 1, :]
        router[...] = small_in[8 : 8 + experts_all, :]
        counts[...] = small_in[8 + ep : 8 + ep + local, 0:2]
        for i in range(count):
            loads[i].wait()
            long[i][...] = short[i][...].astype(F32)
            copies.append(pltpu.make_async_copy(long[i], high_out[i], sem.at[2 + count + i]))
            copies[-1].start()
        for i, target in enumerate((out_to, gtok_to)):
            through[i].wait()
            copies.append(pltpu.make_async_copy(held[i], target, sem.at[i]))
            copies[-1].start()
        for copy in copies:
            copy.wait()

    sds = jax.ShapeDtypeStruct
    hbm = pl.BlockSpec(memory_space=pl.ANY)
    vmem = pl.BlockSpec(memory_space=pltpu.VMEM)
    full = pl.pallas_call(
        kernel,
        out_shape=(
            sds(out.shape, BF16),
            sds(gtok.shape, F32),
            *[sds((1, wide), F32)] * 6,
            sds((experts_all, wide), F32),
            sds((local, 2), F32),
            *[sds(v.shape, F32) for v in low],
        ),
        in_specs=[hbm, hbm, vmem] + [hbm] * len(low),
        out_specs=(hbm, hbm) + (vmem,) * 8 + (hbm,) * len(low),
        scratch_shapes=[
            *[pltpu.VMEM(v.shape, BF16) for v in low],
            *[pltpu.VMEM(v.shape, F32) for v in low],
            pltpu.SemaphoreType.DMA((2 + 2 * len(low),)),
            pltpu.VMEM(out.shape, BF16),
            pltpu.VMEM(gtok.shape, F32),
        ],
        compiler_params=pltpu.CompilerParams(vmem_limit_bytes=56 << 20),
    )(*got)
    norms = [v.reshape(wide) for v in full[2:8]]
    router, counts = full[8:10]
    gdn, gup, go, gqkv, geup, gedn = full[10:]
    return (
        *full[:2],
        *norms[:2],
        gqkv,
        go,
        *norms[2:4],
        gup,
        gdn,
        *norms[4:],
        router.T,
        geup,
        gedn,
        counts,
    )


def solution(mesh):
    both = (DP, EXPERT)
    token = P(both, None)
    in_specs = (token, P(both), token, token, token) + (P(),) * 11
    in_specs += (P(EXPERT, None, None),) * 2
    out_specs = (
        token,
        token,
        P(EXPERT),
        P(EXPERT),
        P(EXPERT, None),
        P(EXPERT, None),
        P(EXPERT),
        P(EXPERT),
        P(EXPERT, None),
        P(EXPERT, None),
        P(EXPERT),
        P(EXPERT),
        P(EXPERT, None),
        P(EXPERT, DP, None),
        P(EXPERT, DP, None),
        P(EXPERT, None),
    )
    return jax.shard_map(shards, mesh=mesh, in_specs=in_specs, out_specs=out_specs, check_vma=False)
```
